32 devices in a mesh: owner: 4 (over x, core), server: 8 (over z, y).
Axes of the slice: x: 2, y: 2, z: 4, core: 2. Of those that a mesh axis runs over, the one named last changes fastest.
Arguments:
- queries: bfloat16 [8192, 1024], P(('owner', 'server')), may hold values from -8 to 8
- key_vectors: bfloat16 [8192, 128], P(('owner', 'server')), may hold values from -8 to 8
- value_vectors: bfloat16 [8192, 128], P(('owner', 'server')), may hold values from -6 to 6
- out_grad: bfloat16 [8192, 1024], P(('owner', 'server')), may hold values from -6 to 6
- segments: int32 [8192], replicated, may hold values from 0 to 7, never falling along the last dimension, each value on 1 to 2048 neighbouring positions
- phase_label: int32 [32], P(('owner', 'server')), may hold values 0 or 1
Outputs:
- attn_out: bfloat16 [8192, 1024], P(('owner', 'server'))
- grad_query: bfloat16 [8192, 1024], P(('owner', 'server'))
- grad_key: float32 [8192, 128], P(('owner', 'server'))
- grad_value: float32 [8192, 128], P(('owner', 'server'))
The draws below stay inside these ranges and needn't reach their ends.
All inputs are finite; a program needn't handle non-finite values. No bound on the sum of `phase_label` on one device may be relied on, other than what follows from the above.
Results may differ from the reference program's by a relative error of at most 0.012.
The reference program's roundings to bfloat16 on the way (of `weights` and `grad_score`) count: a program that leaves them out, or rounds other values in their place, can miss the bound.
Values may be sent and summed in bfloat16 or wider, within the bound.
No kernel may reach another device: no remote copies, remote signals or barrier semaphores. Data moves between devices by JAX's collectives and lax.ppermute only.
A program may use at most 128 MiB of HBM per device.

```python
import math
import jax
import jax.numpy as jnp
import numpy as np
from jax import lax

HEAD = 128
QHEADS = 8
TOK_DEV = 256
REACH = 8
TOKENS = 8192
DEVICES = 32


def draw_key_vectors(key, part):
    base = jnp.clip(jax.random.normal(jax.random.fold_in(key, 3), (TOKENS, HEAD), jnp.float32), -6.0, 6.0)
    return base.astype(jnp.bfloat16)


def draw_queries(key, part):
    base = jnp.clip(jax.random.normal(jax.random.fold_in(key, 5), (TOKENS, QHEADS * HEAD), jnp.float32), -6.0, 6.0)
    return base.astype(jnp.bfloat16)


def plant(drawn, stream_key, low, high):
    extent = drawn.shape
    spot = [jax.random.randint(jax.random.fold_in(stream_key, axis), (), 0, extent[axis]) for axis in range(len(extent))]
    drawn = drawn.at[tuple(spot)].set(low)
    longest = extent.index(max(extent))
    spot[longest] = (spot[longest] + 1) % extent[longest]
    return drawn.at[tuple(spot)].set(high)


def level_of(stream_key, shape, cuts, smallest, high):
    level = 1.0
    for position, parts in cuts:
        heights = jax.random.uniform(jax.random.fold_in(jax.random.fold_in(stream_key, 6), position), (parts,), jnp.float32, smallest / len(cuts), high / len(cuts))
        level = level * jnp.repeat(jnp.exp(heights), shape[position] // parts).reshape((-1,) + (1,) * (len(shape) - 1 - position))
    return level


def profile(amount, total, bound, lean):
    loads = [(1 << 20) // math.isqrt(grade ** lean) + 1 for grade in range(2, amount + 1)]
    rest, given = total - bound - (amount - 1), [1] * (amount - 1)
    while rest > 0:
        free = [i for i in range(amount - 1) if given[i] < bound]
        mass, left = sum([loads[i] for i in free]), rest
        for i in free:
            more = min(bound - given[i], max(1, left * loads[i] // mass), rest)
            given[i] = given[i] + more
            rest = rest - more
    return np.array([bound] + given)


def uneven_parts(stream_key, count, total, reach, skew):
    if count == 2:
        one = jax.random.randint(stream_key, (), max(1, total - reach), min(reach, total - 1) + 1)
        return jnp.stack([one, total - one])
    sizes = jnp.asarray(profile(count, total, reach, skew), jnp.int32)
    twos = (count - 1) // 2
    donor, receiver = sizes[1:1 + 2 * twos:2], sizes[2:2 + 2 * twos:2]
    room = jnp.minimum(donor - 1, reach - receiver)
    passed = jax.random.randint(jax.random.fold_in(stream_key, 1), (twos,), 0, 1 << 20) % (room + 1)
    sizes = sizes.at[1:1 + 2 * twos:2].set(donor - passed).at[2:2 + 2 * twos:2].set(receiver + passed)
    return sizes[jax.random.permutation(jax.random.fold_in(stream_key, 2), count)]


def noise(stream_key, shape, spread, most, split=(), held_as=jnp.bfloat16):
    drawn = jax.random.normal(stream_key, shape, jnp.float32) * spread
    if len(split) > 0:
        drawn = level_of(stream_key, shape, split, -0.22, 0.18) * drawn
    return jnp.clip(drawn, min=-most, max=most).astype(held_as)


def setup_inputs(seed: int = 0) -> dict:
    key_of = jax.random.split(jax.random.key(seed), 7)
    queries = draw_queries(jax.random.fold_in(key_of[6], 71), 0)
    key_vectors = draw_key_vectors(jax.random.fold_in(key_of[6], 71), 0)
    value_vectors = noise(key_of[2], (TOKENS, HEAD), 1.0, 6.0, ((0, 32),))
    out_grad = noise(key_of[3], (TOKENS, QHEADS * HEAD), 1.0, 6.0, ((0, 32),))
    segments = jnp.searchsorted(jnp.cumsum(uneven_parts(key_of[4], 2 * TOKENS // (REACH * TOK_DEV), TOKENS, REACH * TOK_DEV, 1)), jnp.arange(TOKENS), side="right").astype(jnp.int32)
    phase_label = plant((jax.random.randint(key_of[5], (DEVICES,), 0, 2) < 1).astype(jnp.int32), jax.random.fold_in(key_of[5], 1), 0, 1)
    return {"queries": queries, "key_vectors": key_vectors, "value_vectors": value_vectors, "out_grad": out_grad, "segments": segments, "phase_label": phase_label}


def tile_pass(query_tile, grad_tile, key_window, value_window, allowed, pong_flag):
    score_scale = HEAD ** -0.5
    outputs = []
    query_grads = []
    key_grad = jnp.zeros(key_window.shape, jnp.float32)
    value_grad = jnp.zeros(value_window.shape, jnp.float32)
    for head_index in range(QHEADS):
        query_head = query_tile[:, head_index * HEAD:(head_index + 1) * HEAD]
        grad_head = grad_tile[:, head_index * HEAD:(head_index + 1) * HEAD]
        score = jnp.dot(query_head, key_window.T, preferred_element_type=jnp.float32) * score_scale
        score = jnp.where(allowed, score, -1e30)
        row_top = jnp.max(score, axis=1, keepdims=True)
        expos = jnp.exp(score - row_top)
        row_total = jnp.sum(expos, axis=1, keepdims=True)
        weights = expos.astype(jnp.bfloat16)
        head_out = jnp.dot(weights, value_window, preferred_element_type=jnp.float32) / row_total
        out_rounded = head_out.astype(jnp.bfloat16)
        outputs.append(out_rounded)
        row_delta = jnp.sum(grad_head.astype(jnp.float32) * out_rounded.astype(jnp.float32), axis=1, keepdims=True)
        probs_full = expos / row_total
        grad_prob = jnp.dot(grad_head, value_window.T, preferred_element_type=jnp.float32)
        grad_score = (probs_full * (grad_prob - row_delta) * score_scale).astype(jnp.bfloat16)
        query_grads.append(jnp.dot(grad_score, key_window, preferred_element_type=jnp.float32) * pong_flag)
        key_grad = key_grad + jnp.dot(grad_score.T, query_head, preferred_element_type=jnp.float32) * pong_flag
        value_grad = value_grad + jnp.dot(probs_full.astype(jnp.bfloat16).T, grad_head, preferred_element_type=jnp.float32) * pong_flag
    return jnp.concatenate(outputs, axis=1), jnp.concatenate(query_grads, axis=1).astype(jnp.bfloat16), key_grad, value_grad


def reference(queries, key_vectors, value_vectors, out_grad, segments, phase_label):
    tiles = TOKENS // TOK_DEV
    key_span = (REACH + 1) * TOK_DEV
    pad_rows = REACH * TOK_DEV
    keys_padded = jnp.concatenate([jnp.zeros((pad_rows, HEAD), key_vectors.dtype), key_vectors], axis=0)
    values_padded = jnp.concatenate([jnp.zeros((pad_rows, HEAD), value_vectors.dtype), value_vectors], axis=0)
    segs_padded = jnp.concatenate([jnp.full((pad_rows,), -1, jnp.int32), segments.astype(jnp.int32)], axis=0)
    causal = jnp.arange(key_span)[None, :] <= jnp.arange(TOK_DEV)[:, None] + pad_rows

    def scan_step(carried, tile_index):
        key_total, value_total = carried
        row_start = (tile_index * TOK_DEV).astype(jnp.int32)
        query_tile = lax.dynamic_slice_in_dim(queries, row_start, TOK_DEV, 0)
        grad_tile = lax.dynamic_slice_in_dim(out_grad, row_start, TOK_DEV, 0)
        key_window = lax.dynamic_slice_in_dim(keys_padded, row_start, key_span, 0)
        value_window = lax.dynamic_slice_in_dim(values_padded, row_start, key_span, 0)
        key_segs = lax.dynamic_slice_in_dim(segs_padded, row_start, key_span, 0)
        query_segs = lax.dynamic_slice_in_dim(segments.astype(jnp.int32), row_start, TOK_DEV, 0)
        allowed = causal & (query_segs[:, None] == key_segs[None, :])
        pong_flag = lax.dynamic_slice_in_dim(phase_label, tile_index, 1, 0).astype(jnp.float32)[0]
        tile_out, tile_dq, key_grad, value_grad = tile_pass(query_tile, grad_tile, key_window, value_window, allowed, pong_flag)
        old_key = lax.dynamic_slice_in_dim(key_total, row_start, key_span, 0)
        old_value = lax.dynamic_slice_in_dim(value_total, row_start, key_span, 0)
        key_total = lax.dynamic_update_slice_in_dim(key_total, old_key + key_grad, row_start, 0)
        value_total = lax.dynamic_update_slice_in_dim(value_total, old_value + value_grad, row_start, 0)
        return (key_total, value_total), (tile_out, tile_dq)

    initial = (jnp.zeros((TOKENS + pad_rows, HEAD), jnp.float32), jnp.zeros((TOKENS + pad_rows, HEAD), jnp.float32))
    totals, stacked = lax.scan(scan_step, initial, jnp.arange(tiles, dtype=jnp.int32))
    attn_out = stacked[0].reshape(TOKENS, QHEADS * HEAD)
    grad_query = stacked[1].reshape(TOKENS, QHEADS * HEAD)
    return attn_out, grad_query, totals[0][pad_rows:], totals[1][pad_rows:]
```

```python
import functools
import math

import jax
import jax.numpy as jnp
from jax import lax
from jax.experimental import pallas as pl
from jax.experimental.pallas import tpu as pltpu
from jax.sharding import PartitionSpec as P

REACH = 8
NEG = -1e30
AXES = ("owner", "server")
NT = (((1,), (1,)), ((), ()))
NN = (((1,), (0,)), ((), ()))


def dot(a, b, dims=NN):
    return lax.dot_general(a, b, dims, preferred_element_type=jnp.float32)


def attend(heads, tok, width, slots, *refs):
    flags, pong = refs[0], refs[1]
    q_ref, g_ref, start_ref = refs[2:5]
    kv_refs = refs[5 : 6 + slots]
    out_ref, dq_ref, own_ref = refs[6 + slots : 9 + slots]
    part_refs = refs[9 + slots : 9 + 2 * slots]
    qs, gs, acc, top, total, delta, p_buf, d_buf, dq_acc, tiles, parts = refs[9 + 2 * slots :]
    scale = width**-0.5
    c = scale * math.log2(math.e)

    for h in range(heads):
        qs[h * tok : (h + 1) * tok, :] = q_ref[:, h * width : (h + 1) * width]
        gs[h * tok : (h + 1) * tok, :] = g_ref[:, h * width : (h + 1) * width]

    def masked(s, rel):
        rows = lax.broadcasted_iota(jnp.int32, (tok, tok), 0)
        ok = rows >= start_ref[0:1, :] - rel
        if isinstance(rel, int):
            ok = ok & (rows <= lax.broadcasted_iota(jnp.int32, (tok, tok), 1))
        return jnp.where(ok, s, NEG)

    def forward(kv, rel, mask, first):
        k = kv[:, :width]
        vt = kv[:, width:].T
        for h in range(heads):
            lanes = slice(h * tok, (h + 1) * tok)
            s = dot(k, qs[lanes, :], NT)
            if mask:
                s = masked(s, rel)
            m = jnp.max(s, axis=0, keepdims=True)
            if not first:
                m = jnp.maximum(m, top[0:1, lanes])
            p = jnp.exp2(s * c - m * c)
            t = jnp.sum(p, axis=0, keepdims=True)
            o = dot(vt, p.astype(jnp.bfloat16))
            if first:
                total[0:1, lanes] = t
                acc[:, lanes] = o
            else:
                alpha = jnp.exp2((top[0:1, lanes] - m) * c)
                total[0:1, lanes] = total[0:1, lanes] * alpha + t
                acc[:, lanes] = acc[:, lanes] * alpha + o
            top[0:1, lanes] = m

    def backward(kv, rel, mask, first):
        k = kv[:, :width]
        v = kv[:, width:]
        kt = k.T
        for h in range(heads):
            lanes = slice(h * tok, (h + 1) * tok)
            s = dot(k, qs[lanes, :], NT)
            if mask:
                s = masked(s, rel)
            p = jnp.exp2(s * c - top[0:1, lanes])
            dp = dot(v, gs[lanes, :], NT)
            ds = (p * (dp - delta[0:1, lanes])).astype(jnp.bfloat16)
            p_buf[:, lanes] = p.astype(jnp.bfloat16)
            d_buf[:, lanes] = ds
            part = dot(kt, ds)
            if first:
                dq_acc[:, lanes] = part
            else:
                dq_acc[:, lanes] += part
        return dot(d_buf[...], qs[...]) * scale, dot(p_buf[...], gs[...])

    for i in range(slots + 1):
        tiles[i] = kv_refs[i][...]

    def each_seen(visit):
        def step(i, carry):
            @pl.when(flags[0, i] == 2)
            def _():
                visit(i, flags[1, i], False)

            @pl.when(flags[0, i] == 1)
            def _():
                visit(i, flags[1, i], True)

            return carry

        lax.fori_loop(0, slots, step, 0)

    forward(tiles[slots], REACH * tok, True, True)
    each_seen(lambda i, rel, mask: forward(tiles[i], rel, mask, False))

    for h in range(heads):
        lanes = slice(h * tok, (h + 1) * tok)
        cols = slice(h * width, (h + 1) * width)
        o = (acc[:, lanes] / total[0:1, lanes]).T.astype(jnp.bfloat16)
        out_ref[:, cols] = o
        prod = g_ref[:, cols].astype(jnp.float32) * o.astype(jnp.float32)
        delta[0:1, lanes] = jnp.sum(prod.T, axis=0, keepdims=True)
        top[0:1, lanes] = top[0:1, lanes] * c + jnp.log2(total[0:1, lanes])

    @pl.when(pong[0] == 1)
    def _():
        dk, dv = backward(tiles[slots], REACH * tok, True, True)
        own_ref[:, :width] = dk
        own_ref[:, width:] = dv
        parts[...] = jnp.zeros_like(parts)

        def visit(i, rel, mask):
            dk, dv = backward(tiles[i], rel, mask, False)
            parts[i, :, :width] = dk.astype(jnp.bfloat16)
            parts[i, :, width:] = dv.astype(jnp.bfloat16)

        each_seen(visit)
        for i in range(slots):
            part_refs[i][...] = parts[i]

        for h in range(heads):
            lanes = slice(h * tok, (h + 1) * tok)
            cols = slice(h * width, (h + 1) * width)
            dq_ref[:, cols] = (dq_acc[:, lanes] * scale).T.astype(jnp.bfloat16)

    @pl.when(pong[0] != 1)
    def _():
        dq_ref[...] = jnp.zeros_like(dq_ref)
        own_ref[...] = jnp.zeros_like(own_ref)
        for i in range(slots):
            part_refs[i][...] = jnp.zeros_like(part_refs[i])


def run_attend(flags, pong, queries, out_grad, start, tiles, width):
    tok = queries.shape[0]
    heads = queries.shape[1] // width
    slots = len(tiles) - 1
    rows = heads * tok
    vmem = pl.BlockSpec(memory_space=pltpu.VMEM)
    smem = pl.BlockSpec(memory_space=pltpu.SMEM)
    bf, f32 = jnp.bfloat16, jnp.float32
    big = jax.ShapeDtypeStruct(queries.shape, bf)
    pairs = 2 * rows * (slots + 1) * tok
    return pl.pallas_call(
        functools.partial(attend, heads, tok, width, slots),
        out_shape=[big, big, jax.ShapeDtypeStruct((tok, 2 * width), f32)]
        + [jax.ShapeDtypeStruct((tok, 2 * width), bf)] * slots,
        in_specs=[smem, smem] + [vmem] * (3 + slots + 1),
        out_specs=[vmem] * (3 + slots),
        scratch_shapes=[
            pltpu.VMEM((rows, width), bf),
            pltpu.VMEM((rows, width), bf),
            pltpu.VMEM((width, rows), f32),
            pltpu.VMEM((8, rows), f32),
            pltpu.VMEM((8, rows), f32),
            pltpu.VMEM((8, rows), f32),
            pltpu.VMEM((tok, rows), bf),
            pltpu.VMEM((tok, rows), bf),
            pltpu.VMEM((width, rows), f32),
            pltpu.VMEM((slots + 1, tok, 2 * width), bf),
            pltpu.VMEM((slots, tok, 2 * width), bf),
        ],
        compiler_params=pltpu.CompilerParams(vmem_limit_bytes=48 * 1024 * 1024),
        cost_estimate=pl.CostEstimate(
            flops=7 * pairs * width, bytes_accessed=8 << 20, transcendentals=pairs
        ),
    )(flags, pong, queries, out_grad, start, *tiles)


def on_device(queries, key_vectors, value_vectors, out_grad, segments, phase_label):
    tok, width = key_vectors.shape
    span = (REACH + 1) * tok
    devices = lax.axis_size(AXES)
    me = lax.axis_index(AXES)
    place = lax.rem(me, REACH)
    kv = jnp.concatenate([key_vectors, value_vectors], axis=1)

    def swap(block, bit):
        return lax.ppermute(block, AXES, [(i, i ^ bit) for i in range(devices)])

    def shift(block, by):
        pairs = [(i, i + by) for i in range(devices) if 0 <= i + by < devices]
        return lax.ppermute(block, AXES, pairs)

    def later(bit):
        return (place ^ bit) > place

    before = shift(kv, REACH)
    slot = {0: before}
    for bit in (4, 6, 2, 1):
        slot[bit] = swap(jnp.where(later(bit), kv, before), bit)
    for bit in (4, 6, 2):
        slot[bit ^ 1] = swap(slot[bit], 1)
    order = list(range(REACH))

    padded = jnp.concatenate([jnp.full((REACH * tok,), -1, jnp.int32), segments], axis=0)
    key_segs = lax.dynamic_slice_in_dim(padded, me * tok, span, 0)
    my_segs = key_segs[REACH * tok :]
    start = jnp.sum((key_segs[:, None] < my_segs[None, :]).astype(jnp.int32), axis=0, dtype=jnp.int32)
    back = jnp.array([lax.rem(place - (place ^ b) + 2 * REACH - 1, REACH) + 1 for b in order])
    rel = (REACH - back) * tok
    first, last = start[0], start[tok - 1]
    seen = (rel + tok > first).astype(jnp.int32) + (rel >= last).astype(jnp.int32)
    flags = jnp.stack([seen, rel])
    out = run_attend(
        flags, phase_label, queries, out_grad, start[None, :], [slot[b] for b in order] + [kv], width
    )
    attn_out, grad_query, own = out[:3]
    part = dict(zip(order, out[3:], strict=True))

    f32, bf = jnp.float32, jnp.bfloat16
    mine, others = own, part[0].astype(f32)
    for bit in (4, 6, 2):
        got = swap(part[bit ^ 1], 1)
        pair = (part[bit].astype(f32) + got.astype(f32)).astype(bf)
        came = swap(pair, bit).astype(f32)
        mine = mine + jnp.where(later(bit), came, 0.0)
        others = others + jnp.where(later(bit), 0.0, came)
    came = swap(part[1], 1).astype(f32)
    mine = mine + jnp.where(later(1), came, 0.0)
    others = others + jnp.where(later(1), 0.0, came)
    mine = mine + shift(others.astype(bf), -REACH).astype(f32)
    return (attn_out, grad_query, mine[:, :width], mine[:, width:])


def solution(mesh):
    rows = P(AXES, None)
    return jax.shard_map(
        on_device,
        mesh=mesh,
        in_specs=(rows, rows, rows, rows, P(), P(AXES)),
        out_specs=(rows, rows, rows, rows),
        check_vma=False,
    )
```

```python
import functools
import math

import jax
import jax.numpy as jnp
from jax import lax
from jax.experimental import pallas as pl
from jax.experimental.pallas import tpu as pltpu
from jax.sharding import PartitionSpec as P

REACH = 8
NEG = -1e30
AXES = ("owner", "server")
NT = (((1,), (1,)), ((), ()))
NN = (((1,), (0,)), ((), ()))


def dot(a, b, dims=NN):
    return lax.dot_general(a, b, dims, preferred_element_type=jnp.float32)


def attend(heads, tok, width, slots, *refs):
    flags, pong = refs[0], refs[1]
    q_ref, g_ref, start_ref = refs[2:5]
    kv_refs = refs[5 : 6 + slots]
    out_ref, dq_ref, own_ref = refs[6 + slots : 9 + slots]
    part_refs = refs[9 + slots : 9 + 2 * slots]
    qs, gs, acc, top, total, delta, p_buf, d_buf, dq_acc, tiles, parts, s_buf = refs[9 + 2 * slots :]
    scale = width**-0.5
    c = scale * math.log2(math.e)

    for h in range(heads):
        qs[h * tok : (h + 1) * tok, :] = q_ref[:, h * width : (h + 1) * width]
        gs[h * tok : (h + 1) * tok, :] = g_ref[:, h * width : (h + 1) * width]

    groups = tok // 8

    def masked(s, rel, own):
        rows = lax.broadcasted_iota(jnp.int32, (tok, tok), 0)
        ok = rows >= start_ref[0:1, :] - rel
        if own:
            ok = ok & (rows <= lax.broadcasted_iota(jnp.int32, (tok, tok), 1))
        return jnp.where(ok, s, NEG)

    def scores(i, rel, mask, own):
        k = tiles[i, :, :width]
        for h in range(heads):
            lanes = slice(h * tok, (h + 1) * tok)
            s = dot(k, qs[lanes, :], NT) * c
            if mask:
                s = masked(s, rel, own)
            s_buf[i, :, lanes] = s
            m = jnp.max(s.reshape(groups, 8, tok), axis=0)
            top[:, lanes] = m if own else jnp.maximum(top[:, lanes], m)

    def forward(i, own):
        vt = tiles[i, :, width:].T
        for h in range(heads):
            lanes = slice(h * tok, (h + 1) * tok)
            p = jnp.exp2(s_buf[i, :, lanes] - top[0:1, lanes])
            t = jnp.sum(p.reshape(groups, 8, tok), axis=0)
            p_buf[:, lanes] = p.astype(jnp.bfloat16)
            total[:, lanes] = t if own else total[:, lanes] + t
        o = dot(vt, p_buf[...])
        acc[...] = o if own else acc[...] + o

    def backward(i, own):
        v = tiles[i, :, width:]
        kt = tiles[i, :, :width].T
        for h in range(heads):
            lanes = slice(h * tok, (h + 1) * tok)
            p = jnp.exp2(s_buf[i, :, lanes] - top[0:1, lanes])
            dp = dot(v, gs[lanes, :], NT)
            ds = (p * (dp - delta[0:1, lanes])).astype(jnp.bfloat16)
            p_buf[:, lanes] = p.astype(jnp.bfloat16)
            d_buf[:, lanes] = ds
        part = dot(kt, d_buf[...])
        dq_acc[...] = part if own else dq_acc[...] + part
        return dot(d_buf[...], qs[...]) * scale, dot(p_buf[...], gs[...])

    for i in range(slots + 1):
        tiles[i] = kv_refs[i][...]

    def each_seen(visit):
        def step(i, carry):
            @pl.when(flags[0, i] > 0)
            def _():
                visit(i)

            return carry

        lax.fori_loop(0, slots, step, 0)

    scores(slots, REACH * tok, True, True)
    each_seen(lambda i: scores(i, flags[1, i], True, False))
    for h in range(heads):
        lanes = slice(h * tok, (h + 1) * tok)
        top[0:1, lanes] = jnp.max(top[:, lanes], axis=0, keepdims=True)
    forward(slots, True)
    each_seen(lambda i: forward(i, False))

    for h in range(heads):
        lanes = slice(h * tok, (h + 1) * tok)
        cols = slice(h * width, (h + 1) * width)
        sums = jnp.sum(total[:, lanes], axis=0, keepdims=True)
        o = (acc[:, lanes] / sums).T.astype(jnp.bfloat16)
        out_ref[:, cols] = o
        prod = g_ref[:, cols].astype(jnp.float32) * o.astype(jnp.float32)
        delta[0:1, lanes] = jnp.sum(prod.T, axis=0, keepdims=True)
        top[0:1, lanes] = top[0:1, lanes] + jnp.log2(sums)

    @pl.when(pong[0] == 1)
    def _():
        dk, dv = backward(slots, True)
        own_ref[:, :width] = dk
        own_ref[:, width:] = dv
        parts[...] = jnp.zeros_like(parts)

        def visit(i):
            dk, dv = backward(i, False)
            parts[i, :, :width] = dk.astype(jnp.bfloat16)
            parts[i, :, width:] = dv.astype(jnp.bfloat16)

        each_seen(visit)
        for i in range(slots):
            part_refs[i][...] = parts[i]

        for h in range(heads):
            lanes = slice(h * tok, (h + 1) * tok)
            cols = slice(h * width, (h + 1) * width)
            dq_ref[:, cols] = (dq_acc[:, lanes] * scale).T.astype(jnp.bfloat16)

    @pl.when(pong[0] != 1)
    def _():
        dq_ref[...] = jnp.zeros_like(dq_ref)
        own_ref[...] = jnp.zeros_like(own_ref)
        for i in range(slots):
            part_refs[i][...] = jnp.zeros_like(part_refs[i])


def run_attend(flags, pong, queries, out_grad, start, tiles, width):
    tok = queries.shape[0]
    heads = queries.shape[1] // width
    slots = len(tiles) - 1
    rows = heads * tok
    vmem = pl.BlockSpec(memory_space=pltpu.VMEM)
    smem = pl.BlockSpec(memory_space=pltpu.SMEM)
    bf, f32 = jnp.bfloat16, jnp.float32
    big = jax.ShapeDtypeStruct(queries.shape, bf)
    pairs = 2 * rows * (slots + 1) * tok
    return pl.pallas_call(
        functools.partial(attend, heads, tok, width, slots),
        out_shape=[big, big, jax.ShapeDtypeStruct((tok, 2 * width), f32)]
        + [jax.ShapeDtypeStruct((tok, 2 * width), bf)] * slots,
        in_specs=[smem, smem] + [vmem] * (3 + slots + 1),
        out_specs=[vmem] * (3 + slots),
        scratch_shapes=[
            pltpu.VMEM((rows, width), bf),
            pltpu.VMEM((rows, width), bf),
            pltpu.VMEM((width, rows), f32),
            pltpu.VMEM((8, rows), f32),
            pltpu.VMEM((8, rows), f32),
            pltpu.VMEM((8, rows), f32),
            pltpu.VMEM((tok, rows), bf),
            pltpu.VMEM((tok, rows), bf),
            pltpu.VMEM((width, rows), f32),
            pltpu.VMEM((slots + 1, tok, 2 * width), bf),
            pltpu.VMEM((slots, tok, 2 * width), bf),
            pltpu.VMEM((slots + 1, tok, rows), f32),
        ],
        compiler_params=pltpu.CompilerParams(vmem_limit_bytes=48 * 1024 * 1024),
        cost_estimate=pl.CostEstimate(
            flops=7 * pairs * width, bytes_accessed=8 << 20, transcendentals=pairs
        ),
    )(flags, pong, queries, out_grad, start, *tiles)


def on_device(queries, key_vectors, value_vectors, out_grad, segments, phase_label):
    tok, width = key_vectors.shape
    span = (REACH + 1) * tok
    devices = lax.axis_size(AXES)
    me = lax.axis_index(AXES)
    place = lax.rem(me, REACH)
    kv = jnp.concatenate([key_vectors, value_vectors], axis=1)

    def swap(block, bit):
        return lax.ppermute(block, AXES, [(i, i ^ bit) for i in range(devices)])

    def shift(block, by):
        pairs = [(i, i + by) for i in range(devices) if 0 <= i + by < devices]
        return lax.ppermute(block, AXES, pairs)

    def later(bit):
        return (place ^ bit) > place

    before = shift(kv, REACH)
    slot = {0: before}
    for bit in (4, 6, 2, 1):
        slot[bit] = swap(jnp.where(later(bit), kv, before), bit)
    for bit in (4, 6, 2):
        slot[bit ^ 1] = swap(slot[bit], 1)
    order = list(range(REACH))

    padded = jnp.concatenate([jnp.full((REACH * tok,), -1, jnp.int32), segments], axis=0)
    key_segs = lax.dynamic_slice_in_dim(padded, me * tok, span, 0)
    my_segs = key_segs[REACH * tok :]
    start = jnp.sum((key_segs[:, None] < my_segs[None, :]).astype(jnp.int32), axis=0, dtype=jnp.int32)
    back = jnp.array([lax.rem(place - (place ^ b) + 2 * REACH - 1, REACH) + 1 for b in order])
    rel = (REACH - back) * tok
    first, last = start[0], start[tok - 1]
    seen = (rel + tok > first).astype(jnp.int32) + (rel >= last).astype(jnp.int32)
    flags = jnp.stack([seen, rel])
    out = run_attend(
        flags, phase_label, queries, out_grad, start[None, :], [slot[b] for b in order] + [kv], width
    )
    attn_out, grad_query, own = out[:3]
    part = dict(zip(order, out[3:], strict=True))

    f32, bf = jnp.float32, jnp.bfloat16
    mine, others = own, part[0].astype(f32)
    for bit in (4, 6, 2):
        got = swap(part[bit ^ 1], 1)
        pair = (part[bit].astype(f32) + got.astype(f32)).astype(bf)
        came = swap(pair, bit).astype(f32)
        mine = mine + jnp.where(later(bit), came, 0.0)
        others = others + jnp.where(later(bit), 0.0, came)
    came = swap(part[1], 1).astype(f32)
    mine = mine + jnp.where(later(1), came, 0.0)
    others = others + jnp.where(later(1), 0.0, came)
    mine = mine + shift(others.astype(bf), -REACH).astype(f32)
    return (attn_out, grad_query, mine[:, :width], mine[:, width:])


def solution(mesh):
    rows = P(AXES, None)
    return jax.shard_map(
        on_device,
        mesh=mesh,
        in_specs=(rows, rows, rows, rows, P(), P(AXES)),
        out_specs=(rows, rows, rows, rows),
        check_vma=False,
    )
```

```python
import functools
import math

import jax
import jax.numpy as jnp
from jax import lax
from jax.experimental import pallas as pl
from jax.experimental.pallas import tpu as pltpu
from jax.sharding import PartitionSpec as P

REACH = 8
NEG = -1e30
AXES = ("owner", "server")
NT = (((1,), (1,)), ((), ()))
NN = (((1,), (0,)), ((), ()))
BF = jnp.bfloat16
F32 = jnp.float32
VMEM = pl.BlockSpec(memory_space=pltpu.VMEM)
SMEM = pl.BlockSpec(memory_space=pltpu.SMEM)


def room(mib):
    return pltpu.CompilerParams(vmem_limit_bytes=mib << 20)


OWN = -1
NEAR = ((0, OWN), (4, 6, 2, 1))


def dot(a, b, dims=NN):
    return lax.dot_general(a, b, dims, preferred_element_type=F32)


def pack_pair(k_ref, v_ref, kv_ref, sems):
    width = k_ref.shape[1]
    copies = [
        pltpu.make_async_copy(src, kv_ref.at[:, pl.ds(i * width, width)], sems.at[i])
        for i, src in enumerate((k_ref, v_ref))
    ]
    for copy in copies:
        copy.start()
    for copy in copies:
        copy.wait()


def choose(place_ref, kv_ref, before_ref, *outs):
    for bit, out in zip((4, 2, 1), outs, strict=True):
        ahead = (place_ref[0] & bit) == 0

        @pl.when(ahead)
        def _():
            out[...] = kv_ref[...]

        @pl.when(jnp.logical_not(ahead))
        def _():
            out[...] = before_ref[...]


def document_starts(me_ref, seg_ref, start_ref, first_ref):
    lanes = seg_ref.shape[1]
    tok = start_ref.shape[1]
    base = pl.multiple_of(me_ref[0] * (tok // lanes), tok // lanes)
    row = jnp.concatenate([seg_ref[pl.ds(base + j, 1), :] for j in range(tok // lanes)], axis=1)
    grid = jnp.broadcast_to(row, (tok, tok))
    inside = jnp.sum((grid.T < grid).astype(jnp.int32), axis=0, keepdims=True)
    head = jnp.sum((seg_ref[...] < row[0, 0]).astype(jnp.int32)) - me_ref[0] * tok
    start_ref[...] = jnp.where(inside > 0, inside, head)
    first_ref[0] = head


def tile_views(ctx, place, bit):
    if bit == OWN:
        return 0
    back = ((place - (place ^ bit) + 2 * REACH - 1) & (REACH - 1)) + 1
    return -back * ctx.tok


class Sizes:
    def __init__(self, heads, tok, width):
        self.heads, self.tok, self.width = heads, tok, width
        self.rows = heads * tok
        self.scale = width**-0.5
        self.c = self.scale * math.log2(math.e)

    def lanes(self, h):
        return slice(h * self.tok, (h + 1) * self.tok)

    def cols(self, h):
        return slice(h * self.width, (h + 1) * self.width)


def stack_heads(z, src, dst):
    for h in range(z.heads):
        dst[z.lanes(h), :] = src[:, z.cols(h)]


def masked(z, s, start_ref, rel, own):
    rows = lax.broadcasted_iota(jnp.int32, (z.tok, z.tok), 0)
    ok = rows >= start_ref[0:1, :] - rel
    if own:
        ok = ok & (rows <= lax.broadcasted_iota(jnp.int32, (z.tok, z.tok), 1))
    return jnp.where(ok, s, NEG)


def backward_tile(z, tile, prob, qs, gs, delta, p_buf, d_buf, dq_acc, fresh):
    v = tile[:, z.width :]
    kt = tile[:, : z.width].T
    for h in range(z.heads):
        lanes = z.lanes(h)
        p = prob(h)
        dp = dot(v, gs[lanes, :], NT)
        d_buf[:, lanes] = (p * (dp - delta[0:1, lanes])).astype(BF)
        p_buf[:, lanes] = p.astype(BF)
    part = dot(kt, d_buf[...])
    dq_acc[...] = part if fresh else dq_acc[...] + part
    return dot(d_buf[...], qs[...]) * z.scale, dot(p_buf[...], gs[...])


def forward_kernel(z, order, fresh, early, *refs):
    refs = list(refs)
    place_ref, first_ref, pong, q_ref = refs[:4]
    g_ref = refs.pop(4) if early else None
    start_ref = refs[4]
    n = len(order)
    at = 5
    if not fresh:
        old_top, old_total, old_acc = refs[at : at + 3]
        at += 3
    kv_refs = refs[at : at + n]
    at += n
    if early:
        out_ref, top, delta, dq_acc = refs[at : at + 4]
        at += 4
        part_refs = refs[at : at + early]
        at += early
        total, acc, gs, d_buf = refs[at : at + 4]
        at += 4
    else:
        top, total, acc = refs[at : at + 3]
        at += 3
    qs, p_buf, tiles, s_buf = refs[at:]
    groups = z.tok // 8
    loop = n - 1 if fresh else n
    stack_heads(z, q_ref, qs)
    for i in range(n):
        tiles[i] = kv_refs[i][...]

    def scores(i, rel, own):
        k = tiles[i, :, : z.width]
        for h in range(z.heads):
            lanes = z.lanes(h)
            s = masked(z, dot(k, qs[lanes, :], NT) * z.c, start_ref, rel, own)
            s_buf[i, :, lanes] = s
            m = jnp.max(s.reshape(groups, 8, z.tok), axis=0)
            top[:, lanes] = m if own else jnp.maximum(top[:, lanes], m)

    def forward(i, own):
        vt = tiles[i, :, z.width :].T
        for h in range(z.heads):
            lanes = z.lanes(h)
            p = jnp.exp2(s_buf[i, :, lanes] - top[0:1, lanes])
            t = jnp.sum(p.reshape(groups, 8, z.tok), axis=0)
            p_buf[:, lanes] = p.astype(BF)
            total[:, lanes] = t if own else total[:, lanes] + t
        o = dot(vt, p_buf[...])
        acc[...] = o if own else acc[...] + o

    place = place_ref[0]
    rels = [tile_views(z, place, bit) for bit in order]

    def each_seen(visit):
        def step(i, carry):
            rel = rels[0]
            for j in range(1, loop):
                rel = jnp.where(i == j, rels[j], rel)

            @pl.when(rel + z.tok > first_ref[0])
            def _():
                visit(i, rel)

            return carry

        lax.fori_loop(0, loop, step, 0)

    if fresh:
        scores(n - 1, 0, True)
    else:
        top[...] = jnp.broadcast_to(old_top[0:1, :], top.shape)
    each_seen(lambda i, rel: scores(i, rel, False))
    top[0:1, :] = jnp.max(top[...], axis=0, keepdims=True)
    if fresh:
        forward(n - 1, True)
    else:
        alpha = jnp.exp2(old_top[0:1, :] - top[0:1, :])
        total[...] = old_total[...] * alpha
        acc[...] = old_acc[...] * alpha
    each_seen(lambda i, rel: forward(i, False))
    if not early:
        return

    for h in range(z.heads):
        lanes = z.lanes(h)
        sums = jnp.sum(total[:, lanes], axis=0, keepdims=True)
        o = (acc[:, lanes] / sums).T.astype(BF)
        out_ref[:, z.cols(h)] = o
        prod = g_ref[:, z.cols(h)].astype(F32) * o.astype(F32)
        delta[0:1, lanes] = jnp.sum(prod.T, axis=0, keepdims=True)
        top[0:1, lanes] = top[0:1, lanes] + jnp.log2(sums)

    dq_acc[...] = jnp.zeros_like(dq_acc)
    for part in part_refs:
        part[...] = jnp.zeros_like(part)

    @pl.when(pong[0] == 1)
    def _():
        stack_heads(z, g_ref, gs)
        for i in range(early):

            @pl.when(rels[i] + z.tok > first_ref[0])
            def _():
                def prob(h):
                    return jnp.exp2(s_buf[i, :, z.lanes(h)] - top[0:1, z.lanes(h)])

                dk, dv = backward_tile(z, kv_refs[i], prob, qs, gs, delta, p_buf, d_buf, dq_acc, False)
                part_refs[i][:, : z.width] = dk.astype(BF)
                part_refs[i][:, z.width :] = dv.astype(BF)


def backward_kernel(z, order, last, *refs):
    place_ref, first_ref, pong = refs[:3]
    q_ref, g_ref, start_ref, top, delta, dq_in = refs[3:9]
    n = len(order)
    kv_refs = refs[9 : 9 + n]
    out_ref = refs[9 + n]
    part_refs = refs[10 + n : 10 + 2 * n]
    qs, gs, p_buf, d_buf = refs[10 + 2 * n : 14 + 2 * n]
    dq_acc = refs[14 + 2 * n] if last else out_ref
    place = place_ref[0]

    @pl.when(pong[0] == 1)
    def _():
        stack_heads(z, q_ref, qs)
        stack_heads(z, g_ref, gs)
        dq_acc[...] = dq_in[...]
        for i, bit in enumerate(order):
            rel = tile_views(z, place, bit)
            seen = rel + z.tok > first_ref[0]

            @pl.when(seen)
            def _():
                def prob(h):
                    s = dot(kv_refs[i][:, : z.width], qs[z.lanes(h), :], NT) * z.c
                    s = masked(z, s, start_ref, rel, bit == OWN)
                    return jnp.exp2(s - top[0:1, z.lanes(h)])

                dk, dv = backward_tile(z, kv_refs[i], prob, qs, gs, delta, p_buf, d_buf, dq_acc, False)
                part_refs[i][:, : z.width] = dk.astype(part_refs[i].dtype)
                part_refs[i][:, z.width :] = dv.astype(part_refs[i].dtype)

            @pl.when(jnp.logical_not(seen))
            def _():
                part_refs[i][...] = jnp.zeros_like(part_refs[i])

        if last:
            for h in range(z.heads):
                out_ref[:, z.cols(h)] = (dq_acc[:, z.lanes(h)] * z.scale).T.astype(BF)

    @pl.when(pong[0] != 1)
    def _():
        out_ref[...] = jnp.zeros_like(out_ref)
        for part in part_refs:
            part[...] = jnp.zeros_like(part)


def cost(z, tiles, products):
    pairs = z.rows * tiles * z.tok
    return pl.CostEstimate(
        flops=2 * products * pairs * z.width, bytes_accessed=6 << 20, transcendentals=pairs
    )


def run_forward(z, scalars, queries, out_grad, start, state, tiles, order, early):
    n = len(order)
    shape = jax.ShapeDtypeStruct
    stats, wide = shape((8, z.rows), F32), shape((z.width, z.rows), F32)
    scratch = [
        pltpu.VMEM((z.rows, z.width), BF),
        pltpu.VMEM((z.tok, z.rows), BF),
        pltpu.VMEM((n, z.tok, 2 * z.width), BF),
        pltpu.VMEM((n, z.tok, z.rows), F32),
    ]
    if early:
        outs = [shape(queries.shape, BF), stats, stats, wide] + [shape((z.tok, 2 * z.width), BF)] * early
        scratch = [
            pltpu.VMEM((8, z.rows), F32),
            pltpu.VMEM((z.width, z.rows), F32),
            pltpu.VMEM((z.rows, z.width), BF),
            pltpu.VMEM((z.tok, z.rows), BF),
        ] + scratch
    else:
        outs = [stats, stats, wide]
    args = [queries, out_grad, start] if early else [queries, start]
    args += list(state) + list(tiles)
    return pl.pallas_call(
        functools.partial(forward_kernel, z, order, not state, early),
        out_shape=outs,
        in_specs=[SMEM] * 3 + [VMEM] * len(args),
        out_specs=[VMEM] * len(outs),
        scratch_shapes=scratch,
        compiler_params=room(24 if early else 16),
        cost_estimate=cost(z, n, 4),
    )(*scalars, *args)


def run_backward(z, scalars, queries, out_grad, start, state, tiles, order, last):
    n = len(order)
    shape = jax.ShapeDtypeStruct
    dq = shape(queries.shape, BF) if last else shape((z.width, z.rows), F32)
    parts = [shape((z.tok, 2 * z.width), F32 if bit == OWN else BF) for bit in order]
    return pl.pallas_call(
        functools.partial(backward_kernel, z, order, last),
        out_shape=[dq] + parts,
        in_specs=[SMEM] * 3 + [VMEM] * (6 + n),
        out_specs=[VMEM] * (1 + n),
        scratch_shapes=[
            pltpu.VMEM((z.rows, z.width), BF),
            pltpu.VMEM((z.rows, z.width), BF),
            pltpu.VMEM((z.tok, z.rows), BF),
            pltpu.VMEM((z.tok, z.rows), BF),
        ]
        + ([pltpu.VMEM((z.width, z.rows), F32)] if last else []),
        compiler_params=room(10),
        cost_estimate=cost(z, n, 10),
    )(*scalars, queries, out_grad, start, *state, *tiles)


def on_device(queries, key_vectors, value_vectors, out_grad, segments, phase_label):
    tok, width = key_vectors.shape
    z = Sizes(queries.shape[1] // width, tok, width)
    devices = lax.axis_size(AXES)
    me = lax.axis_index(AXES).astype(jnp.int32)
    place = me & (REACH - 1)
    shape = jax.ShapeDtypeStruct
    block = shape((tok, 2 * width), BF)

    def swap(x, bit):
        return lax.ppermute(x, AXES, [(i, i ^ bit) for i in range(devices)])

    def shift(x, by):
        pairs = [(i, i + by) for i in range(devices) if 0 <= i + by < devices]
        return lax.ppermute(x, AXES, pairs)

    def give_back(x, bit):
        pairs = [(i, i ^ bit if i & bit else (i ^ bit) - REACH) for i in range(devices)]
        return lax.ppermute(x, AXES, [(i, j) for i, j in pairs if j >= 0])

    kv = pl.pallas_call(
        pack_pair,
        out_shape=block,
        in_specs=[pl.BlockSpec(memory_space=pltpu.HBM)] * 2,
        out_specs=VMEM,
        scratch_shapes=[pltpu.SemaphoreType.DMA((2,))],
        compiler_params=room(4),
    )(key_vectors, value_vectors)
    before = shift(kv, REACH)
    start, first = pl.pallas_call(
        document_starts,
        out_shape=[shape((1, tok), jnp.int32), shape((1,), jnp.int32)],
        in_specs=[SMEM, VMEM],
        out_specs=[VMEM, SMEM],
        compiler_params=room(4),
    )(me[None], segments.reshape(-1, 128))
    ahead = pl.pallas_call(
        choose, out_shape=[block] * 3, in_specs=[SMEM] + [VMEM] * 2, out_specs=[VMEM] * 3, compiler_params=room(4)
    )(place[None], kv, before)
    slot = {0: before, 4: swap(ahead[0], 4), 2: swap(ahead[1], 2)}
    slot[1] = swap(ahead[2], 1)
    slot[5] = swap(slot[4], 1)
    slot[6] = swap(slot[4], 2)
    slot[3] = swap(slot[2], 1)
    slot[7] = swap(slot[5], 2)

    scalars = (place[None], first, phase_label)
    slot[OWN] = kv
    state = ()
    for near in NEAR:
        state = run_forward(z, scalars, queries, None, start, state, [slot[b] for b in near], near, 0)
    order = (5, 7, 3)
    attn_out, top, delta, dq, *parts = run_forward(
        z, scalars, queries, out_grad, start, state, [slot[b] for b in order], order, 3
    )
    part = dict(zip(order, parts, strict=True))
    got = {b: swap(part[b ^ 1], 1) for b in (4, 6, 2)}
    some = (4, 6, 2)
    dq, *parts = run_backward(
        z, scalars, queries, out_grad, start, (top, delta, dq), [slot[b] for b in some], some, False
    )
    part.update(zip(some, parts, strict=True))

    def pair(bit):
        return (part[bit].astype(F32) + got[bit].astype(F32)).astype(BF)

    dq, *ready = lax.optimization_barrier((dq, *(pair(b) for b in some)))
    came = {bit: swap(x, bit) for bit, x in zip(some, ready, strict=True)}
    rest = (1, 0, OWN)
    grad_query, *parts = run_backward(
        z, scalars, queries, out_grad, start, (top, delta, dq), [slot[b] for b in rest], rest, True
    )
    part.update(zip(rest, parts, strict=True))
    mine = part[OWN]
    others = part[0].astype(F32)
    for bits in ((4, 6), (2,)):
        total = sum(came[b].astype(F32) for b in bits)
        behind = (place & bits[0]) == 0
        mine = mine + jnp.where(behind, total, 0.0)
        others = others + jnp.where(behind, 0.0, total)
    last = [give_back(part[1], 1), shift(others.astype(BF), -REACH)]
    mine = mine + sum(x.astype(F32) for x in last)
    return (attn_out, grad_query, mine[:, :width], mine[:, width:])


def solution(mesh):
    rows = P(AXES, None)
    return jax.shard_map(
        on_device,
        mesh=mesh,
        in_specs=(rows, rows, rows, rows, P(), P(AXES)),
        out_specs=(rows, rows, rows, rows),
        check_vma=False,
    )
```

```python
import functools
import math

import jax
import jax.numpy as jnp
from jax import lax
from jax.experimental import pallas as pl
from jax.experimental.pallas import tpu as pltpu
from jax.sharding import PartitionSpec as P

REACH = 8
NEG = -1e30
AXES = ("owner", "server")
NT = (((1,), (1,)), ((), ()))
NN = (((1,), (0,)), ((), ()))
BF = jnp.bfloat16
F32 = jnp.float32
VMEM = pl.BlockSpec(memory_space=pltpu.VMEM)
SMEM = pl.BlockSpec(memory_space=pltpu.SMEM)


def room(mib):
    return pltpu.CompilerParams(vmem_limit_bytes=mib << 20)


OWN = -1
NEAR = ((0, OWN), (4, 2, 1))


def dot(a, b, dims=NN):
    return lax.dot_general(a, b, dims, preferred_element_type=F32)


def pack_pair(k_ref, v_ref, kv_ref, sems):
    width = k_ref.shape[1]
    copies = [
        pltpu.make_async_copy(src, kv_ref.at[:, pl.ds(i * width, width)], sems.at[i])
        for i, src in enumerate((k_ref, v_ref))
    ]
    for copy in copies:
        copy.start()
    for copy in copies:
        copy.wait()


def choose(place_ref, kv_ref, before_ref, *outs):
    for bit, out in zip((4, 2, 1), outs, strict=True):
        ahead = (place_ref[0] & bit) == 0

        @pl.when(ahead)
        def _():
            out[...] = kv_ref[...]

        @pl.when(jnp.logical_not(ahead))
        def _():
            out[...] = before_ref[...]


def finish(place_ref, own_ref, far_refs, last_refs, key_ref, value_ref):
    width = key_ref.shape[1]
    key_ref[...] = own_ref[:, :width]
    value_ref[...] = own_ref[:, width:]

    def add(refs):
        key_ref[...] += sum(r[:, :width].astype(F32) for r in refs)
        value_ref[...] += sum(r[:, width:].astype(F32) for r in refs)

    for bits, refs in far_refs:
        pl.when((place_ref[0] & bits) == 0)(functools.partial(add, refs))
    add(last_refs)


def document_starts(me_ref, seg_ref, start_ref, first_ref):
    lanes = seg_ref.shape[1]
    tok = start_ref.shape[1]
    base = pl.multiple_of(me_ref[0] * (tok // lanes), tok // lanes)
    row = jnp.concatenate([seg_ref[pl.ds(base + j, 1), :] for j in range(tok // lanes)], axis=1)
    grid = jnp.broadcast_to(row, (tok, tok))
    inside = jnp.sum((grid.T < grid).astype(jnp.int32), axis=0, keepdims=True)
    head = jnp.sum((seg_ref[...] < row[0, 0]).astype(jnp.int32)) - me_ref[0] * tok
    start_ref[...] = jnp.where(inside > 0, inside, head)
    first_ref[0] = head


def tile_views(ctx, place, bit):
    if bit == OWN:
        return 0
    back = ((place - (place ^ bit) + 2 * REACH - 1) & (REACH - 1)) + 1
    return -back * ctx.tok


class Sizes:
    def __init__(self, heads, tok, width):
        self.heads, self.tok, self.width = heads, tok, width
        self.rows = heads * tok
        self.scale = width**-0.5
        self.c = self.scale * math.log2(math.e)

    def lanes(self, h):
        return slice(h * self.tok, (h + 1) * self.tok)

    def cols(self, h):
        return slice(h * self.width, (h + 1) * self.width)


def stack_heads(z, src, dst):
    for h in range(z.heads):
        dst[z.lanes(h), :] = src[:, z.cols(h)]


def masked(z, s, start_ref, rel, own):
    rows = lax.broadcasted_iota(jnp.int32, (z.tok, z.tok), 0)
    ok = rows >= start_ref[0:1, :] - rel
    if own:
        ok = ok & (rows <= lax.broadcasted_iota(jnp.int32, (z.tok, z.tok), 1))
    return jnp.where(ok, s, NEG)


def backward_tile(z, tile, prob, qs, gs, delta, p_buf, d_buf, dq_acc):
    v = tile[:, z.width :]
    kt = tile[:, : z.width].T
    for h in range(z.heads):
        lanes = z.lanes(h)
        p = prob(h)
        dp = dot(v, gs[lanes, :], NT)
        d_buf[:, lanes] = (p * (dp - delta[0:1, lanes])).astype(BF)
        p_buf[:, lanes] = p.astype(BF)
    dv = dot(p_buf[...], gs[...])
    dk = dot(d_buf[...], qs[...]) * z.scale
    dq_acc[...] += dot(kt, d_buf[...])
    return dk, dv


def forward_kernel(z, order, fresh, early, *refs):
    refs = list(refs)
    place_ref, first_ref, pong, q_ref = refs[:4]
    g_ref = refs.pop(4) if early else None
    start_ref = refs[4]
    n = len(order)
    at = 5
    if not fresh:
        old_top, old_total, old_acc = refs[at : at + 3]
        at += 3
    kv_refs = refs[at : at + n]
    at += n
    if early:
        out_ref, top, delta, dq_acc = refs[at : at + 4]
        at += 4
        part_refs = refs[at : at + early]
        at += early
        total, acc, gs, d_buf = refs[at : at + 4]
        at += 4
    else:
        top, total, acc = refs[at : at + 3]
        at += 3
    qs, p_buf, tiles, s_buf = refs[at:]
    groups = z.tok // 8
    loop = n - 1 if fresh else n
    stack_heads(z, q_ref, qs)
    for i in range(n):
        tiles[i] = kv_refs[i][...]

    def scores(i, rel, own):
        k = tiles[i, :, : z.width]
        for h in range(z.heads):
            lanes = z.lanes(h)
            s = masked(z, dot(k, qs[lanes, :], NT) * z.c, start_ref, rel, own)
            s_buf[i, :, lanes] = s
            m = jnp.max(s.reshape(groups, 8, z.tok), axis=0)
            top[:, lanes] = m if own else jnp.maximum(top[:, lanes], m)

    def forward(i, own):
        vt = tiles[i, :, z.width :].T
        for h in range(z.heads):
            lanes = z.lanes(h)
            p = jnp.exp2(s_buf[i, :, lanes] - top[0:1, lanes])
            t = jnp.sum(p.reshape(groups, 8, z.tok), axis=0)
            p_buf[:, lanes] = p.astype(BF)
            total[:, lanes] = t if own else total[:, lanes] + t
        o = dot(vt, p_buf[...])
        acc[...] = o if own else acc[...] + o

    place = place_ref[0]
    rels = [tile_views(z, place, bit) for bit in order]

    def each_seen(visit):
        def step(i, carry):
            rel = rels[0]
            for j in range(1, loop):
                rel = jnp.where(i == j, rels[j], rel)

            @pl.when(rel + z.tok > first_ref[0])
            def _():
                visit(i, rel)

            return carry

        lax.fori_loop(0, loop, step, 0)

    if fresh:
        scores(n - 1, 0, True)
    else:
        top[...] = jnp.broadcast_to(old_top[0:1, :], top.shape)
    each_seen(lambda i, rel: scores(i, rel, False))
    top[0:1, :] = jnp.max(top[...], axis=0, keepdims=True)
    if fresh:
        forward(n - 1, True)
    else:
        alpha = jnp.exp2(old_top[0:1, :] - top[0:1, :])
        total[...] = old_total[...] * alpha
        acc[...] = old_acc[...] * alpha
    each_seen(lambda i, rel: forward(i, False))
    if not early:
        return

    for h in range(z.heads):
        lanes = z.lanes(h)
        sums = jnp.sum(total[:, lanes], axis=0, keepdims=True)
        o = (acc[:, lanes] / sums).T.astype(BF)
        out_ref[:, z.cols(h)] = o
        prod = g_ref[:, z.cols(h)].astype(F32) * o.astype(F32)
        delta[0:1, lanes] = jnp.sum(prod.T, axis=0, keepdims=True)
        top[0:1, lanes] = top[0:1, lanes] + jnp.log2(sums)

    dq_acc[...] = jnp.zeros_like(dq_acc)
    for part in part_refs:
        part[...] = jnp.zeros_like(part)

    @pl.when(pong[0] == 1)
    def _():
        stack_heads(z, g_ref, gs)
        for i in range(early):

            @pl.when(rels[i] + z.tok > first_ref[0])
            def _():
                def prob(h):
                    return jnp.exp2(s_buf[i, :, z.lanes(h)] - top[0:1, z.lanes(h)])

                dk, dv = backward_tile(z, kv_refs[i], prob, qs, gs, delta, p_buf, d_buf, dq_acc)
                part_refs[i][:, : z.width] = dk.astype(BF)
                part_refs[i][:, z.width :] = dv.astype(BF)


def backward_kernel(z, order, last, *refs):
    place_ref, first_ref, pong = refs[:3]
    q_ref, g_ref, start_ref, top, delta, dq_in = refs[3:9]
    n = len(order)
    kv_refs = refs[9 : 9 + n]
    out_ref = refs[9 + n]
    part_refs = refs[10 + n : 10 + 2 * n]
    qs, gs, p_buf, d_buf = refs[10 + 2 * n : 14 + 2 * n]
    dq_acc = refs[14 + 2 * n] if last else out_ref
    place = place_ref[0]

    @pl.when(pong[0] == 1)
    def _():
        stack_heads(z, q_ref, qs)
        stack_heads(z, g_ref, gs)
        dq_acc[...] = dq_in[...]
        for i, bit in enumerate(order):
            rel = tile_views(z, place, bit)
            seen = rel + z.tok > first_ref[0]

            @pl.when(seen)
            def _():
                def prob(h):
                    s = dot(kv_refs[i][:, : z.width], qs[z.lanes(h), :], NT) * z.c
                    s = masked(z, s, start_ref, rel, bit == OWN)
                    return jnp.exp2(s - top[0:1, z.lanes(h)])

                dk, dv = backward_tile(z, kv_refs[i], prob, qs, gs, delta, p_buf, d_buf, dq_acc)
                part_refs[i][:, : z.width] = dk.astype(part_refs[i].dtype)
                part_refs[i][:, z.width :] = dv.astype(part_refs[i].dtype)

            @pl.when(jnp.logical_not(seen))
            def _():
                part_refs[i][...] = jnp.zeros_like(part_refs[i])

        if last:
            for h in range(z.heads):
                out_ref[:, z.cols(h)] = (dq_acc[:, z.lanes(h)] * z.scale).T.astype(BF)

    @pl.when(pong[0] != 1)
    def _():
        out_ref[...] = jnp.zeros_like(out_ref)
        for part in part_refs:
            part[...] = jnp.zeros_like(part)


def cost(z, tiles, products):
    pairs = z.rows * tiles * z.tok
    return pl.CostEstimate(
        flops=2 * products * pairs * z.width, bytes_accessed=6 << 20, transcendentals=pairs
    )


def run_forward(z, scalars, queries, out_grad, start, state, tiles, order, early):
    n = len(order)
    shape = jax.ShapeDtypeStruct
    stats, wide = shape((8, z.rows), F32), shape((z.width, z.rows), F32)
    scratch = [
        pltpu.VMEM((z.rows, z.width), BF),
        pltpu.VMEM((z.tok, z.rows), BF),
        pltpu.VMEM((n, z.tok, 2 * z.width), BF),
        pltpu.VMEM((n, z.tok, z.rows), F32),
    ]
    if early:
        outs = [shape(queries.shape, BF), stats, stats, wide] + [shape((z.tok, 2 * z.width), BF)] * early
        scratch = [
            pltpu.VMEM((8, z.rows), F32),
            pltpu.VMEM((z.width, z.rows), F32),
            pltpu.VMEM((z.rows, z.width), BF),
            pltpu.VMEM((z.tok, z.rows), BF),
        ] + scratch
    else:
        outs = [stats, stats, wide]
    args = [queries, out_grad, start] if early else [queries, start]
    args += list(state) + list(tiles)
    return pl.pallas_call(
        functools.partial(forward_kernel, z, order, not state, early),
        out_shape=outs,
        in_specs=[SMEM] * 3 + [VMEM] * len(args),
        out_specs=[VMEM] * len(outs),
        scratch_shapes=scratch,
        compiler_params=room(24 if early else 16),
        cost_estimate=cost(z, n, 4),
    )(*scalars, *args)


def run_backward(z, scalars, queries, out_grad, start, state, tiles, order, last):
    n = len(order)
    shape = jax.ShapeDtypeStruct
    dq = shape(queries.shape, BF) if last else shape((z.width, z.rows), F32)
    parts = [shape((z.tok, 2 * z.width), F32 if bit == OWN else BF) for bit in order]
    return pl.pallas_call(
        functools.partial(backward_kernel, z, order, last),
        out_shape=[dq] + parts,
        in_specs=[SMEM] * 3 + [VMEM] * (6 + n),
        out_specs=[VMEM] * (1 + n),
        scratch_shapes=[
            pltpu.VMEM((z.rows, z.width), BF),
            pltpu.VMEM((z.rows, z.width), BF),
            pltpu.VMEM((z.tok, z.rows), BF),
            pltpu.VMEM((z.tok, z.rows), BF),
        ]
        + ([pltpu.VMEM((z.width, z.rows), F32)] if last else []),
        compiler_params=room(10),
        cost_estimate=cost(z, n, 10),
    )(*scalars, queries, out_grad, start, *state, *tiles)


def on_device(queries, key_vectors, value_vectors, out_grad, segments, phase_label):
    tok, width = key_vectors.shape
    z = Sizes(queries.shape[1] // width, tok, width)
    devices = lax.axis_size(AXES)
    me = lax.axis_index(AXES).astype(jnp.int32)
    place = me & (REACH - 1)
    shape = jax.ShapeDtypeStruct
    block = shape((tok, 2 * width), BF)

    def swap(x, bit):
        return lax.ppermute(x, AXES, [(i, i ^ bit) for i in range(devices)])

    def shift(x, by):
        pairs = [(i, i + by) for i in range(devices) if 0 <= i + by < devices]
        return lax.ppermute(x, AXES, pairs)

    def give_back(x, bit):
        pairs = [(i, i ^ bit if i & bit else (i ^ bit) - REACH) for i in range(devices)]
        return lax.ppermute(x, AXES, [(i, j) for i, j in pairs if j >= 0])

    kv = pl.pallas_call(
        pack_pair,
        out_shape=block,
        in_specs=[pl.BlockSpec(memory_space=pltpu.HBM)] * 2,
        out_specs=VMEM,
        scratch_shapes=[pltpu.SemaphoreType.DMA((2,))],
        compiler_params=room(4),
    )(key_vectors, value_vectors)
    before = shift(kv, REACH)
    start, first = pl.pallas_call(
        document_starts,
        out_shape=[shape((1, tok), jnp.int32), shape((1,), jnp.int32)],
        in_specs=[SMEM, VMEM],
        out_specs=[VMEM, SMEM],
        compiler_params=room(4),
    )(me[None], segments.reshape(-1, 128))
    before, start, first = lax.optimization_barrier((before, start, first))
    ahead = pl.pallas_call(
        choose, out_shape=[block] * 3, in_specs=[SMEM] + [VMEM] * 2, out_specs=[VMEM] * 3, compiler_params=room(4)
    )(place[None], kv, before)
    slot = {0: before, 4: swap(ahead[0], 4), 2: swap(ahead[1], 2)}
    slot[1] = swap(ahead[2], 1)
    scalars = (place[None], first, phase_label)
    slot[OWN] = kv

    def more(state, near):
        return run_forward(z, scalars, queries, None, start, state, [slot[b] for b in near], near, 0)

    slot[4], *state = lax.optimization_barrier((slot[4], *more((), NEAR[0])))
    slot[5] = swap(slot[4], 1)
    slot[6] = swap(slot[4], 2)
    slot[3] = swap(slot[2], 1)
    slot[7] = swap(slot[5], 2)
    state = more(state, NEAR[1])
    order = (5, 7, 3, 6)
    attn_out, top, delta, dq, *parts = run_forward(
        z, scalars, queries, out_grad, start, state, [slot[b] for b in order], order, 3
    )
    part = dict(zip(order[:3], parts, strict=True))
    got = {b: swap(part[b ^ 1], 1) for b in (4, 6, 2)}
    some = (4, 6, 2)
    dq, *parts = run_backward(
        z, scalars, queries, out_grad, start, (top, delta, dq), [slot[b] for b in some], some, False
    )
    part.update(zip(some, parts, strict=True))

    def pair(bit):
        return (part[bit].astype(F32) + got[bit].astype(F32)).astype(BF)

    dq, *ready = lax.optimization_barrier((dq, *(pair(b) for b in some)))
    came = {bit: swap(x, bit) for bit, x in zip(some, ready, strict=True)}
    rest = (1, 0, OWN)
    grad_query, *parts = run_backward(
        z, scalars, queries, out_grad, start, (top, delta, dq), [slot[b] for b in rest], rest, True
    )
    part.update(zip(rest, parts, strict=True))
    others = part[0].astype(F32)
    for bits in ((4, 6), (2,)):
        total = sum(came[b].astype(F32) for b in bits)
        others = others + jnp.where((place & bits[0]) == 0, 0.0, total)
    last = [give_back(part[1], 1), shift(others.astype(BF), -REACH)]
    grad_key, grad_value = pl.pallas_call(
        lambda place_ref, own, c4, c6, c2, l1, l0, *outs: finish(
            place_ref, own, ((4, (c4, c6)), (2, (c2,))), (l1, l0), *outs
        ),
        out_shape=[shape((tok, width), F32)] * 2,
        in_specs=[SMEM] + [VMEM] * 6,
        out_specs=[VMEM] * 2,
        compiler_params=room(4),
    )(place[None], part[OWN], came[4], came[6], came[2], *last)
    return (attn_out, grad_query, grad_key, grad_value)


def solution(mesh):
    rows = P(AXES, None)
    return jax.shard_map(
        on_device,
        mesh=mesh,
        in_specs=(rows, rows, rows, rows, P(), P(AXES)),
        out_specs=(rows, rows, rows, rows),
        check_vma=False,
    )
```

```python
import functools
import math

import jax
import jax.numpy as jnp
from jax import lax
from jax.experimental import pallas as pl
from jax.experimental.pallas import tpu as pltpu
from jax.sharding import PartitionSpec as P

REACH = 8
NEG = -1e30
AXES = ("owner", "server")
NT = (((1,), (1,)), ((), ()))
NN = (((1,), (0,)), ((), ()))
BF = jnp.bfloat16
F32 = jnp.float32
VMEM = pl.BlockSpec(memory_space=pltpu.VMEM)
SMEM = pl.BlockSpec(memory_space=pltpu.SMEM)


def room(mib):
    return pltpu.CompilerParams(vmem_limit_bytes=mib << 20)


OWN = -1
NEAR = ((0, OWN), (4, 2, 1))


def dot(a, b, dims=NN):
    return lax.dot_general(a, b, dims, preferred_element_type=F32)


def pack_pair(k_ref, v_ref, kv_ref, sems):
    width = k_ref.shape[1]
    copies = [
        pltpu.make_async_copy(src, kv_ref.at[:, pl.ds(i * width, width)], sems.at[i])
        for i, src in enumerate((k_ref, v_ref))
    ]
    for copy in copies:
        copy.start()
    for copy in copies:
        copy.wait()


def choose(place_ref, kv_ref, before_ref, *outs):
    for bit, out in zip((4, 2, 1), outs, strict=True):
        ahead = (place_ref[0] & bit) == 0

        @pl.when(ahead)
        def _():
            out[...] = kv_ref[...]

        @pl.when(jnp.logical_not(ahead))
        def _():
            out[...] = before_ref[...]


def finish(place_ref, own_ref, far_refs, last_refs, key_ref, value_ref):
    width = key_ref.shape[1]
    key_ref[...] = own_ref[:, :width]
    value_ref[...] = own_ref[:, width:]

    def add(refs):
        key_ref[...] += sum(r[:, :width].astype(F32) for r in refs)
        value_ref[...] += sum(r[:, width:].astype(F32) for r in refs)

    for bits, refs in far_refs:
        pl.when((place_ref[0] & bits) == 0)(functools.partial(add, refs))
    add(last_refs)


def document_starts(me_ref, seg_ref, start_ref, first_ref):
    lanes = seg_ref.shape[1]
    tok = start_ref.shape[1]
    base = pl.multiple_of(me_ref[0] * (tok // lanes), tok // lanes)
    row = jnp.concatenate([seg_ref[pl.ds(base + j, 1), :] for j in range(tok // lanes)], axis=1)
    grid = jnp.broadcast_to(row, (tok, tok))
    inside = jnp.sum((grid.T < grid).astype(jnp.int32), axis=0, keepdims=True)
    head = jnp.sum((seg_ref[...] < row[0, 0]).astype(jnp.int32)) - me_ref[0] * tok
    start_ref[...] = jnp.where(inside > 0, inside, head)
    first_ref[0] = head


def tile_views(ctx, place, bit):
    if bit == OWN:
        return 0
    back = ((place - (place ^ bit) + 2 * REACH - 1) & (REACH - 1)) + 1
    return -back * ctx.tok


class Sizes:
    def __init__(self, heads, tok, width):
        self.heads, self.tok, self.width = heads, tok, width
        self.rows = heads * tok
        self.scale = width**-0.5
        self.c = self.scale * math.log2(math.e)

    def lanes(self, h):
        return slice(h * self.tok, (h + 1) * self.tok)

    def cols(self, h):
        return slice(h * self.width, (h + 1) * self.width)


def stack_heads(z, src, dst):
    for h in range(z.heads):
        dst[z.lanes(h), :] = src[:, z.cols(h)]


def masked(z, s, start_ref, rel, own):
    rows = lax.broadcasted_iota(jnp.int32, (z.tok, z.tok), 0)
    ok = rows >= start_ref[0:1, :] - rel
    if own:
        ok = ok & (rows <= lax.broadcasted_iota(jnp.int32, (z.tok, z.tok), 1))
    return jnp.where(ok, s, NEG)


def backward_tile(z, tile, prob, qs, gs, delta, p_buf, d_buf, dq_acc):
    v = tile[:, z.width :]
    kt = tile[:, : z.width].T
    for h in range(z.heads):
        lanes = z.lanes(h)
        p = prob(h)
        dp = dot(v, gs[lanes, :], NT)
        d_buf[:, lanes] = (p * (dp - delta[0:1, lanes])).astype(BF)
        p_buf[:, lanes] = p.astype(BF)
    dv = dot(p_buf[...], gs[...])
    dk = dot(d_buf[...], qs[...]) * z.scale
    dq_acc[...] += dot(kt, d_buf[...])
    return dk, dv


def forward_kernel(z, order, fresh, early, *refs):
    refs = list(refs)
    place_ref, first_ref, pong, q_ref = refs[:4]
    g_ref = refs.pop(4) if early else None
    start_ref = refs[4]
    n = len(order)
    at = 5
    if not fresh:
        old_top, old_total, old_acc = refs[at : at + 3]
        at += 3
    kv_refs = refs[at : at + n]
    at += n
    if early:
        out_ref, top, delta, dq_acc = refs[at : at + 4]
        at += 4
        part_refs = refs[at : at + early]
        at += early
        total, acc, gs, d_buf = refs[at : at + 4]
        at += 4
    else:
        top, total, acc = refs[at : at + 3]
        at += 3
    qs, p_buf, tiles, s_buf = refs[at:]
    groups = z.tok // 8
    loop = n - 1 if fresh else n
    stack_heads(z, q_ref, qs)
    for i in range(n):
        tiles[i] = kv_refs[i][...]

    def scores(i, rel, own):
        k = tiles[i, :, : z.width]
        for h in range(z.heads):
            lanes = z.lanes(h)
            s = masked(z, dot(k, qs[lanes, :], NT) * z.c, start_ref, rel, own)
            s_buf[i, :, lanes] = s
            m = jnp.max(s.reshape(groups, 8, z.tok), axis=0)
            top[:, lanes] = m if own else jnp.maximum(top[:, lanes], m)

    def forward(i, own):
        vt = tiles[i, :, z.width :].T
        for h in range(z.heads):
            lanes = z.lanes(h)
            p = jnp.exp2(s_buf[i, :, lanes] - top[0:1, lanes])
            t = jnp.sum(p.reshape(groups, 8, z.tok), axis=0)
            p_buf[:, lanes] = p.astype(BF)
            total[:, lanes] = t if own else total[:, lanes] + t
        o = dot(vt, p_buf[...])
        acc[...] = o if own else acc[...] + o

    place = place_ref[0]
    rels = [tile_views(z, place, bit) for bit in order]

    def each_seen(visit):
        def step(i, carry):
            rel = rels[0]
            for j in range(1, loop):
                rel = jnp.where(i == j, rels[j], rel)

            @pl.when(rel + z.tok > first_ref[0])
            def _():
                visit(i, rel)

            return carry

        lax.fori_loop(0, loop, step, 0)

    if fresh:
        scores(n - 1, 0, True)
    else:
        top[...] = jnp.broadcast_to(old_top[0:1, :], top.shape)
    each_seen(lambda i, rel: scores(i, rel, False))
    top[0:1, :] = jnp.max(top[...], axis=0, keepdims=True)
    if fresh:
        forward(n - 1, True)
    else:
        alpha = jnp.exp2(old_top[0:1, :] - top[0:1, :])
        total[...] = old_total[...] * alpha
        acc[...] = old_acc[...] * alpha
    each_seen(lambda i, rel: forward(i, False))
    if not early:
        return

    for h in range(z.heads):
        lanes = z.lanes(h)
        sums = jnp.sum(total[:, lanes], axis=0, keepdims=True)
        o = (acc[:, lanes] / sums).T.astype(BF)
        out_ref[:, z.cols(h)] = o
        prod = g_ref[:, z.cols(h)].astype(F32) * o.astype(F32)
        delta[0:1, lanes] = jnp.sum(prod.T, axis=0, keepdims=True)
        top[0:1, lanes] = top[0:1, lanes] + jnp.log2(sums)

    dq_acc[...] = jnp.zeros_like(dq_acc)
    for part in part_refs:
        part[...] = jnp.zeros_like(part)

    @pl.when(pong[0] == 1)
    def _():
        stack_heads(z, g_ref, gs)
        for i in range(early):

            @pl.when(rels[i] + z.tok > first_ref[0])
            def _():
                def prob(h):
                    return jnp.exp2(s_buf[i, :, z.lanes(h)] - top[0:1, z.lanes(h)])

                dk, dv = backward_tile(z, kv_refs[i], prob, qs, gs, delta, p_buf, d_buf, dq_acc)
                part_refs[i][:, : z.width] = dk.astype(BF)
                part_refs[i][:, z.width :] = dv.astype(BF)


def backward_kernel(z, order, last, *refs):
    place_ref, first_ref, pong = refs[:3]
    q_ref, g_ref, start_ref, top, delta, dq_in = refs[3:9]
    n = len(order)
    kv_refs = refs[9 : 9 + n]
    out_ref = refs[9 + n]
    part_refs = refs[10 + n : 10 + 2 * n]
    qs, gs, p_buf, d_buf = refs[10 + 2 * n : 14 + 2 * n]
    dq_acc = refs[14 + 2 * n] if last else out_ref
    place = place_ref[0]

    @pl.when(pong[0] == 1)
    def _():
        stack_heads(z, q_ref, qs)
        stack_heads(z, g_ref, gs)
        dq_acc[...] = dq_in[...]
        for i, bit in enumerate(order):
            rel = tile_views(z, place, bit)
            seen = rel + z.tok > first_ref[0]

            @pl.when(seen)
            def _():
                def prob(h):
                    s = dot(kv_refs[i][:, : z.width], qs[z.lanes(h), :], NT) * z.c
                    s = masked(z, s, start_ref, rel, bit == OWN)
                    return jnp.exp2(s - top[0:1, z.lanes(h)])

                dk, dv = backward_tile(z, kv_refs[i], prob, qs, gs, delta, p_buf, d_buf, dq_acc)
                part_refs[i][:, : z.width] = dk.astype(part_refs[i].dtype)
                part_refs[i][:, z.width :] = dv.astype(part_refs[i].dtype)

            @pl.when(jnp.logical_not(seen))
            def _():
                part_refs[i][...] = jnp.zeros_like(part_refs[i])

        if last:
            for h in range(z.heads):
                out_ref[:, z.cols(h)] = (dq_acc[:, z.lanes(h)] * z.scale).T.astype(BF)

    @pl.when(pong[0] != 1)
    def _():
        out_ref[...] = jnp.zeros_like(out_ref)
        for part in part_refs:
            part[...] = jnp.zeros_like(part)


def cost(z, tiles, products):
    pairs = z.rows * tiles * z.tok
    return pl.CostEstimate(
        flops=2 * products * pairs * z.width, bytes_accessed=6 << 20, transcendentals=pairs
    )


def run_forward(z, scalars, queries, out_grad, start, state, tiles, order, early):
    n = len(order)
    shape = jax.ShapeDtypeStruct
    stats, wide = shape((8, z.rows), F32), shape((z.width, z.rows), F32)
    scratch = [
        pltpu.VMEM((z.rows, z.width), BF),
        pltpu.VMEM((z.tok, z.rows), BF),
        pltpu.VMEM((n, z.tok, 2 * z.width), BF),
        pltpu.VMEM((n, z.tok, z.rows), F32),
    ]
    if early:
        outs = [shape(queries.shape, BF), stats, stats, wide] + [shape((z.tok, 2 * z.width), BF)] * early
        scratch = [
            pltpu.VMEM((8, z.rows), F32),
            pltpu.VMEM((z.width, z.rows), F32),
            pltpu.VMEM((z.rows, z.width), BF),
            pltpu.VMEM((z.tok, z.rows), BF),
        ] + scratch
    else:
        outs = [stats, stats, wide]
    args = [queries, out_grad, start] if early else [queries, start]
    args += list(state) + list(tiles)
    return pl.pallas_call(
        functools.partial(forward_kernel, z, order, not state, early),
        out_shape=outs,
        in_specs=[SMEM] * 3 + [VMEM] * len(args),
        out_specs=[VMEM] * len(outs),
        scratch_shapes=scratch,
        compiler_params=room(24 if early else 16),
        cost_estimate=cost(z, n, 4),
    )(*scalars, *args)


def run_backward(z, scalars, queries, out_grad, start, state, tiles, order, last):
    n = len(order)
    shape = jax.ShapeDtypeStruct
    dq = shape(queries.shape, BF) if last else shape((z.width, z.rows), F32)
    parts = [shape((z.tok, 2 * z.width), F32 if bit == OWN else BF) for bit in order]
    return pl.pallas_call(
        functools.partial(backward_kernel, z, order, last),
        out_shape=[dq] + parts,
        in_specs=[SMEM] * 3 + [VMEM] * (6 + n),
        out_specs=[VMEM] * (1 + n),
        scratch_shapes=[
            pltpu.VMEM((z.rows, z.width), BF),
            pltpu.VMEM((z.rows, z.width), BF),
            pltpu.VMEM((z.tok, z.rows), BF),
            pltpu.VMEM((z.tok, z.rows), BF),
        ]
        + ([pltpu.VMEM((z.width, z.rows), F32)] if last else []),
        compiler_params=room(10),
        cost_estimate=cost(z, n, 10),
    )(*scalars, queries, out_grad, start, *state, *tiles)


def on_device(queries, key_vectors, value_vectors, out_grad, segments, phase_label):
    tok, width = key_vectors.shape
    z = Sizes(queries.shape[1] // width, tok, width)
    devices = lax.axis_size(AXES)
    me = lax.axis_index(AXES).astype(jnp.int32)
    place = me & (REACH - 1)
    shape = jax.ShapeDtypeStruct
    block = shape((tok, 2 * width), BF)

    def swap(x, bit):
        return lax.ppermute(x, AXES, [(i, i ^ bit) for i in range(devices)])

    def shift(x, by):
        pairs = [(i, i + by) for i in range(devices) if 0 <= i + by < devices]
        return lax.ppermute(x, AXES, pairs)

    def give_back(x, bit):
        pairs = [(i, i ^ bit if i & bit else (i ^ bit) - REACH) for i in range(devices)]
        return lax.ppermute(x, AXES, [(i, j) for i, j in pairs if j >= 0])

    kv = pl.pallas_call(
        pack_pair,
        out_shape=block,
        in_specs=[pl.BlockSpec(memory_space=pltpu.HBM)] * 2,
        out_specs=VMEM,
        scratch_shapes=[pltpu.SemaphoreType.DMA((2,))],
        compiler_params=room(4),
    )(key_vectors, value_vectors)
    before = shift(kv, REACH)
    start, first = pl.pallas_call(
        document_starts,
        out_shape=[shape((1, tok), jnp.int32), shape((1,), jnp.int32)],
        in_specs=[SMEM, VMEM],
        out_specs=[VMEM, SMEM],
        compiler_params=room(4),
    )(me[None], segments.reshape(-1, 128))
    before, start, first = lax.optimization_barrier((before, start, first))
    ahead = pl.pallas_call(
        choose, out_shape=[block] * 3, in_specs=[SMEM] + [VMEM] * 2, out_specs=[VMEM] * 3, compiler_params=room(4)
    )(place[None], kv, before)
    slot = {0: before, 4: swap(ahead[0], 4), 2: swap(ahead[1], 2)}
    slot[1] = swap(ahead[2], 1)
    scalars = (place[None], first, phase_label)
    slot[OWN] = kv

    def more(state, near):
        return run_forward(z, scalars, queries, None, start, state, [slot[b] for b in near], near, 0)

    slot[4], *state = lax.optimization_barrier((slot[4], *more((), NEAR[0])))
    slot[5] = swap(slot[4], 1)
    slot[6] = swap(slot[4], 2)
    slot[3] = swap(slot[2], 1)
    slot[7] = swap(slot[5], 2)
    state = more(state, NEAR[1])
    order = (5, 7, 3, 6)
    attn_out, top, delta, dq, *parts = run_forward(
        z, scalars, queries, out_grad, start, state, [slot[b] for b in order], order, 3
    )
    part = dict(zip(order[:3], parts, strict=True))
    got = {b: swap(part[b ^ 1], 1) for b in (2, 6, 4)}
    some = (4, 6, 2)
    dq, *parts = run_backward(
        z, scalars, queries, out_grad, start, (top, delta, dq), [slot[b] for b in some], some, False
    )
    part.update(zip(some, parts, strict=True))

    def pair(bit):
        return (part[bit].astype(F32) + got[bit].astype(F32)).astype(BF)

    came = {4: swap(pair(4), 4), 6: swap(pair(6), 6)}
    dq, near_pair = lax.optimization_barrier((dq, pair(2)))
    came[2] = swap(near_pair, 2)
    rest = (1, 0, OWN)
    grad_query, *parts = run_backward(
        z, scalars, queries, out_grad, start, (top, delta, dq), [slot[b] for b in rest], rest, True
    )
    part.update(zip(rest, parts, strict=True))
    others = part[0].astype(F32)
    for bits in ((4, 6), (2,)):
        total = sum(came[b].astype(F32) for b in bits)
        others = others + jnp.where((place & bits[0]) == 0, 0.0, total)
    last = [give_back(part[1], 1), shift(others.astype(BF), -REACH)]
    grad_key, grad_value = pl.pallas_call(
        lambda place_ref, own, c4, c6, c2, l1, l0, *outs: finish(
            place_ref, own, ((4, (c4, c6)), (2, (c2,))), (l1, l0), *outs
        ),
        out_shape=[shape((tok, width), F32)] * 2,
        in_specs=[SMEM] + [VMEM] * 6,
        out_specs=[VMEM] * 2,
        compiler_params=room(4),
    )(place[None], part[OWN], came[4], came[6], came[2], *last)
    return (attn_out, grad_query, grad_key, grad_value)


def solution(mesh):
    rows = P(AXES, None)
    return jax.shard_map(
        on_device,
        mesh=mesh,
        in_specs=(rows, rows, rows, rows, P(), P(AXES)),
        out_specs=(rows, rows, rows, rows),
        check_vma=False,
    )
```

```python
import functools
import math

import jax
import jax.numpy as jnp
from jax import lax
from jax.experimental import pallas as pl
from jax.experimental.pallas import tpu as pltpu
from jax.sharding import PartitionSpec as P

REACH = 8
NEG = -1e30
AXES = ("owner", "server")
NT = (((1,), (1,)), ((), ()))
NN = (((1,), (0,)), ((), ()))
BF = jnp.bfloat16
F32 = jnp.float32
VMEM = pl.BlockSpec(memory_space=pltpu.VMEM)
SMEM = pl.BlockSpec(memory_space=pltpu.SMEM)


def room(mib):
    return pltpu.CompilerParams(vmem_limit_bytes=mib << 20)


OWN = -1
NEAR = ((0, OWN), (4, 2, 1))


def dot(a, b, dims=NN):
    return lax.dot_general(a, b, dims, preferred_element_type=F32)


def pack_pair(k_ref, v_ref, kv_ref, sems):
    width = k_ref.shape[1]
    copies = [
        pltpu.make_async_copy(src, kv_ref.at[:, pl.ds(i * width, width)], sems.at[i])
        for i, src in enumerate((k_ref, v_ref))
    ]
    for copy in copies:
        copy.start()
    for copy in copies:
        copy.wait()


def choose(place_ref, kv_ref, before_ref, *outs):
    for bit, out in zip((4, 2, 1), outs, strict=True):
        ahead = (place_ref[0] & bit) == 0

        @pl.when(ahead)
        def _():
            out[...] = kv_ref[...]

        @pl.when(jnp.logical_not(ahead))
        def _():
            out[...] = before_ref[...]


def finish(place_ref, own_ref, far_refs, last_refs, key_ref, value_ref):
    width = key_ref.shape[1]
    key_ref[...] = own_ref[:, :width]
    value_ref[...] = own_ref[:, width:]

    def add(refs):
        key_ref[...] += sum(r[:, :width].astype(F32) for r in refs)
        value_ref[...] += sum(r[:, width:].astype(F32) for r in refs)

    for bits, refs in far_refs:
        pl.when((place_ref[0] & bits) == 0)(functools.partial(add, refs))
    add(last_refs)


def document_starts(me_ref, seg_ref, start_ref, first_ref):
    lanes = seg_ref.shape[1]
    tok = start_ref.shape[1]
    base = pl.multiple_of(me_ref[0] * (tok // lanes), tok // lanes)
    row = jnp.concatenate([seg_ref[pl.ds(base + j, 1), :] for j in range(tok // lanes)], axis=1)
    grid = jnp.broadcast_to(row, (tok, tok))
    inside = jnp.sum((grid.T < grid).astype(jnp.int32), axis=0, keepdims=True)
    head = jnp.sum((seg_ref[...] < row[0, 0]).astype(jnp.int32)) - me_ref[0] * tok
    start_ref[...] = jnp.where(inside > 0, inside, head)
    first_ref[0] = head


def tile_views(ctx, place, bit):
    if bit == OWN:
        return 0
    back = ((place - (place ^ bit) + 2 * REACH - 1) & (REACH - 1)) + 1
    return -back * ctx.tok


class Sizes:
    def __init__(self, heads, tok, width):
        self.heads, self.tok, self.width = heads, tok, width
        self.rows = heads * tok
        self.scale = width**-0.5
        self.c = self.scale * math.log2(math.e)

    def lanes(self, h):
        return slice(h * self.tok, (h + 1) * self.tok)

    def cols(self, h):
        return slice(h * self.width, (h + 1) * self.width)


def stack_heads(z, src, dst):
    for h in range(z.heads):
        dst[z.lanes(h), :] = src[:, z.cols(h)]


def masked(z, s, start_ref, rel, own):
    rows = lax.broadcasted_iota(jnp.int32, (z.tok, z.tok), 0)
    ok = rows >= start_ref[0:1, :] - rel
    if own:
        ok = ok & (rows <= lax.broadcasted_iota(jnp.int32, (z.tok, z.tok), 1))
    return jnp.where(ok, s, NEG)


def backward_tile(z, tile, prob, qs, gs, delta, p_buf, d_buf, dq_acc):
    v = tile[:, z.width :]
    kt = tile[:, : z.width].T
    for h in range(z.heads):
        lanes = z.lanes(h)
        p = prob(h)
        dp = dot(v, gs[lanes, :], NT)
        d_buf[:, lanes] = (p * (dp - delta[0:1, lanes])).astype(BF)
        p_buf[:, lanes] = p.astype(BF)
    dv = dot(p_buf[...], gs[...])
    dk = dot(d_buf[...], qs[...]) * z.scale
    dq_acc[...] += dot(kt, d_buf[...])
    return dk, dv


def forward_kernel(z, order, fresh, early, *refs):
    refs = list(refs)
    place_ref, first_ref, pong, q_ref = refs[:4]
    g_ref = refs.pop(4) if early or fresh else None
    start_ref = refs[4]
    n = len(order)
    at = 5
    if not fresh:
        old_top, old_total, old_acc = refs[at : at + 3]
        at += 3
    if early:
        turned = refs[at]
        at += 1
    kv_refs = refs[at : at + n]
    at += n
    if early:
        out_ref, top, delta, dq_acc = refs[at : at + 4]
        at += 4
        part_refs = refs[at : at + early]
        at += early
        total, acc, gs, d_buf = refs[at : at + 4]
        at += 4
    else:
        top, total, acc = refs[at : at + 3]
        at += 3
        if fresh:
            turned = refs[at]
            at += 1
    qs, p_buf, tiles, s_buf = refs[at:]
    groups = z.tok // 8
    loop = n - 1 if fresh else n
    stack_heads(z, q_ref, qs)
    for i in range(n):
        tiles[i] = kv_refs[i][...]

    def scores(i, rel, own):
        k = tiles[i, :, : z.width]
        for h in range(z.heads):
            lanes = z.lanes(h)
            s = masked(z, dot(k, qs[lanes, :], NT) * z.c, start_ref, rel, own)
            s_buf[i, :, lanes] = s
            m = jnp.max(s.reshape(groups, 8, z.tok), axis=0)
            top[:, lanes] = m if own else jnp.maximum(top[:, lanes], m)

    def forward(i, own):
        vt = tiles[i, :, z.width :].T
        for h in range(z.heads):
            lanes = z.lanes(h)
            p = jnp.exp2(s_buf[i, :, lanes] - top[0:1, lanes])
            t = jnp.sum(p.reshape(groups, 8, z.tok), axis=0)
            p_buf[:, lanes] = p.astype(BF)
            total[:, lanes] = t if own else total[:, lanes] + t
        o = dot(vt, p_buf[...])
        acc[...] = o if own else acc[...] + o

    place = place_ref[0]
    rels = [tile_views(z, place, bit) for bit in order]

    def each_seen(visit):
        def step(i, carry):
            rel = rels[0]
            for j in range(1, loop):
                rel = jnp.where(i == j, rels[j], rel)

            @pl.when(rel + z.tok > first_ref[0])
            def _():
                visit(i, rel)

            return carry

        lax.fori_loop(0, loop, step, 0)

    if fresh:
        for h in range(z.heads):
            turned[:, z.lanes(h)] = g_ref[:, z.cols(h)].T
        scores(n - 1, 0, True)
    else:
        top[...] = jnp.broadcast_to(old_top[0:1, :], top.shape)
    each_seen(lambda i, rel: scores(i, rel, False))
    top[0:1, :] = jnp.max(top[...], axis=0, keepdims=True)
    if fresh:
        forward(n - 1, True)
    else:
        alpha = jnp.exp2(old_top[0:1, :] - top[0:1, :])
        total[...] = old_total[...] * alpha
        acc[...] = old_acc[...] * alpha
    each_seen(lambda i, rel: forward(i, False))
    if not early:
        return

    for h in range(z.heads):
        lanes = z.lanes(h)
        sums = jnp.sum(total[:, lanes], axis=0, keepdims=True)
        o = (acc[:, lanes] * (1.0 / sums)).astype(BF)
        out_ref[:, z.cols(h)] = o.T
        prod = turned[:, lanes].astype(F32) * o.astype(F32)
        delta[0:1, lanes] = jnp.sum(prod, axis=0, keepdims=True)
        top[0:1, lanes] = top[0:1, lanes] + jnp.log2(sums)

    dq_acc[...] = jnp.zeros_like(dq_acc)
    for part in part_refs:
        part[...] = jnp.zeros_like(part)

    @pl.when(pong[0] == 1)
    def _():
        stack_heads(z, g_ref, gs)
        for i in range(early):

            @pl.when(rels[i] + z.tok > first_ref[0])
            def _():
                def prob(h):
                    return jnp.exp2(s_buf[i, :, z.lanes(h)] - top[0:1, z.lanes(h)])

                dk, dv = backward_tile(z, kv_refs[i], prob, qs, gs, delta, p_buf, d_buf, dq_acc)
                part_refs[i][:, : z.width] = dk.astype(BF)
                part_refs[i][:, z.width :] = dv.astype(BF)


def backward_kernel(z, order, last, *refs):
    place_ref, first_ref, pong = refs[:3]
    q_ref, g_ref, start_ref, top, delta, dq_in = refs[3:9]
    n = len(order)
    kv_refs = refs[9 : 9 + n]
    out_ref = refs[9 + n]
    part_refs = refs[10 + n : 10 + 2 * n]
    qs, gs, p_buf, d_buf = refs[10 + 2 * n : 14 + 2 * n]
    dq_acc = refs[14 + 2 * n] if last else out_ref
    place = place_ref[0]

    @pl.when(pong[0] == 1)
    def _():
        stack_heads(z, q_ref, qs)
        stack_heads(z, g_ref, gs)
        dq_acc[...] = dq_in[...]
        for i, bit in enumerate(order):
            rel = tile_views(z, place, bit)
            seen = rel + z.tok > first_ref[0]

            @pl.when(seen)
            def _():
                def prob(h):
                    s = dot(kv_refs[i][:, : z.width], qs[z.lanes(h), :], NT) * z.c
                    s = masked(z, s, start_ref, rel, bit == OWN)
                    return jnp.exp2(s - top[0:1, z.lanes(h)])

                dk, dv = backward_tile(z, kv_refs[i], prob, qs, gs, delta, p_buf, d_buf, dq_acc)
                part_refs[i][:, : z.width] = dk.astype(part_refs[i].dtype)
                part_refs[i][:, z.width :] = dv.astype(part_refs[i].dtype)

            @pl.when(jnp.logical_not(seen))
            def _():
                part_refs[i][...] = jnp.zeros_like(part_refs[i])

        if last:
            for h in range(z.heads):
                out_ref[:, z.cols(h)] = (dq_acc[:, z.lanes(h)] * z.scale).astype(BF).T

    @pl.when(pong[0] != 1)
    def _():
        out_ref[...] = jnp.zeros_like(out_ref)
        for part in part_refs:
            part[...] = jnp.zeros_like(part)


def cost(z, tiles, products):
    pairs = z.rows * tiles * z.tok
    return pl.CostEstimate(
        flops=2 * products * pairs * z.width, bytes_accessed=6 << 20, transcendentals=pairs
    )


def run_forward(z, scalars, queries, out_grad, start, state, tiles, order, early):
    n = len(order)
    shape = jax.ShapeDtypeStruct
    stats, wide = shape((8, z.rows), F32), shape((z.width, z.rows), F32)
    scratch = [
        pltpu.VMEM((z.rows, z.width), BF),
        pltpu.VMEM((z.tok, z.rows), BF),
        pltpu.VMEM((n, z.tok, 2 * z.width), BF),
        pltpu.VMEM((n, z.tok, z.rows), F32),
    ]
    if early:
        outs = [shape(queries.shape, BF), stats, stats, wide] + [shape((z.tok, 2 * z.width), BF)] * early
        scratch = [
            pltpu.VMEM((8, z.rows), F32),
            pltpu.VMEM((z.width, z.rows), F32),
            pltpu.VMEM((z.rows, z.width), BF),
            pltpu.VMEM((z.tok, z.rows), BF),
        ] + scratch
    else:
        outs = [stats, stats, wide] + ([] if state else [shape((z.width, z.rows), BF)])
    args = [queries, out_grad, start] if early or not state else [queries, start]
    args += list(state) + list(tiles)
    return pl.pallas_call(
        functools.partial(forward_kernel, z, order, not state, early),
        out_shape=outs,
        in_specs=[SMEM] * 3 + [VMEM] * len(args),
        out_specs=[VMEM] * len(outs),
        scratch_shapes=scratch,
        compiler_params=room(24 if early else 16),
        cost_estimate=cost(z, n, 4),
    )(*scalars, *args)


def run_backward(z, scalars, queries, out_grad, start, state, tiles, order, last):
    n = len(order)
    shape = jax.ShapeDtypeStruct
    dq = shape(queries.shape, BF) if last else shape((z.width, z.rows), F32)
    parts = [shape((z.tok, 2 * z.width), F32 if bit == OWN else BF) for bit in order]
    return pl.pallas_call(
        functools.partial(backward_kernel, z, order, last),
        out_shape=[dq] + parts,
        in_specs=[SMEM] * 3 + [VMEM] * (6 + n),
        out_specs=[VMEM] * (1 + n),
        scratch_shapes=[
            pltpu.VMEM((z.rows, z.width), BF),
            pltpu.VMEM((z.rows, z.width), BF),
            pltpu.VMEM((z.tok, z.rows), BF),
            pltpu.VMEM((z.tok, z.rows), BF),
        ]
        + ([pltpu.VMEM((z.width, z.rows), F32)] if last else []),
        compiler_params=room(10),
        cost_estimate=cost(z, n, 10),
    )(*scalars, queries, out_grad, start, *state, *tiles)


def on_device(queries, key_vectors, value_vectors, out_grad, segments, phase_label):
    tok, width = key_vectors.shape
    z = Sizes(queries.shape[1] // width, tok, width)
    devices = lax.axis_size(AXES)
    me = lax.axis_index(AXES).astype(jnp.int32)
    place = me & (REACH - 1)
    shape = jax.ShapeDtypeStruct
    block = shape((tok, 2 * width), BF)

    def swap(x, bit):
        return lax.ppermute(x, AXES, [(i, i ^ bit) for i in range(devices)])

    def shift(x, by):
        pairs = [(i, i + by) for i in range(devices) if 0 <= i + by < devices]
        return lax.ppermute(x, AXES, pairs)

    def give_back(x, bit):
        pairs = [(i, i ^ bit if i & bit else (i ^ bit) - REACH) for i in range(devices)]
        return lax.ppermute(x, AXES, [(i, j) for i, j in pairs if j >= 0])

    kv = pl.pallas_call(
        pack_pair,
        out_shape=block,
        in_specs=[pl.BlockSpec(memory_space=pltpu.HBM)] * 2,
        out_specs=VMEM,
        scratch_shapes=[pltpu.SemaphoreType.DMA((2,))],
        compiler_params=room(4),
    )(key_vectors, value_vectors)
    before = shift(kv, REACH)
    start, first = pl.pallas_call(
        document_starts,
        out_shape=[shape((1, tok), jnp.int32), shape((1,), jnp.int32)],
        in_specs=[SMEM, VMEM],
        out_specs=[VMEM, SMEM],
        compiler_params=room(4),
    )(me[None], segments.reshape(-1, 128))
    before, start, first = lax.optimization_barrier((before, start, first))
    ahead = pl.pallas_call(
        choose, out_shape=[block] * 3, in_specs=[SMEM] + [VMEM] * 2, out_specs=[VMEM] * 3, compiler_params=room(4)
    )(place[None], kv, before)
    slot = {0: before, 4: swap(ahead[0], 4), 2: swap(ahead[1], 2)}
    slot[1] = swap(ahead[2], 1)
    scalars = (place[None], first, phase_label)
    slot[OWN] = kv

    def more(state, near):
        return run_forward(z, scalars, queries, out_grad, start, state, [slot[b] for b in near], near, 0)

    slot[4], *state, turned = lax.optimization_barrier((slot[4], *more((), NEAR[0])))
    slot[5] = swap(slot[4], 1)
    slot[6] = swap(slot[4], 2)
    slot[3] = swap(slot[2], 1)
    slot[7] = swap(slot[5], 2)
    state = more(state, NEAR[1])
    order = (5, 7, 3, 6)
    attn_out, top, delta, dq, *parts = run_forward(
        z, scalars, queries, out_grad, start, (*state, turned), [slot[b] for b in order], order, 3
    )
    part = dict(zip(order[:3], parts, strict=True))
    got = {b: swap(part[b ^ 1], 1) for b in (2, 6, 4)}
    some = (4, 6, 2)
    dq, *parts = run_backward(
        z, scalars, queries, out_grad, start, (top, delta, dq), [slot[b] for b in some], some, False
    )
    part.update(zip(some, parts, strict=True))

    def pair(bit):
        return (part[bit].astype(F32) + got[bit].astype(F32)).astype(BF)

    came = {4: swap(pair(4), 4), 6: swap(pair(6), 6)}
    dq, near_pair = lax.optimization_barrier((dq, pair(2)))
    came[2] = swap(near_pair, 2)
    rest = (1, 0, OWN)
    grad_query, *parts = run_backward(
        z, scalars, queries, out_grad, start, (top, delta, dq), [slot[b] for b in rest], rest, True
    )
    part.update(zip(rest, parts, strict=True))
    others = part[0].astype(F32)
    for bits in ((4, 6), (2,)):
        total = sum(came[b].astype(F32) for b in bits)
        others = others + jnp.where((place & bits[0]) == 0, 0.0, total)
    last = [give_back(part[1], 1), shift(others.astype(BF), -REACH)]
    grad_key, grad_value = pl.pallas_call(
        lambda place_ref, own, c4, c6, c2, l1, l0, *outs: finish(
            place_ref, own, ((4, (c4, c6)), (2, (c2,))), (l1, l0), *outs
        ),
        out_shape=[shape((tok, width), F32)] * 2,
        in_specs=[SMEM] + [VMEM] * 6,
        out_specs=[VMEM] * 2,
        compiler_params=room(4),
    )(place[None], part[OWN], came[4], came[6], came[2], *last)
    return (attn_out, grad_query, grad_key, grad_value)


def solution(mesh):
    rows = P(AXES, None)
    return jax.shard_map(
        on_device,
        mesh=mesh,
        in_specs=(rows, rows, rows, rows, P(), P(AXES)),
        out_specs=(rows, rows, rows, rows),
        check_vma=False,
    )
```

```python
import functools
import math

import jax
import jax.numpy as jnp
from jax import lax
from jax.experimental import pallas as pl
from jax.experimental.pallas import tpu as pltpu
from jax.sharding import PartitionSpec as P

REACH = 8
NEG = -1e30
AXES = ("owner", "server")
NT = (((1,), (1,)), ((), ()))
NN = (((1,), (0,)), ((), ()))
BF = jnp.bfloat16
F32 = jnp.float32
VMEM = pl.BlockSpec(memory_space=pltpu.VMEM)
SMEM = pl.BlockSpec(memory_space=pltpu.SMEM)


def room(mib):
    return pltpu.CompilerParams(vmem_limit_bytes=mib << 20)


OWN = -1
NEAR = ((0, OWN), (4, 2, 1))


def dot(a, b, dims=NN):
    return lax.dot_general(a, b, dims, preferred_element_type=F32)


def pack_pair(k_ref, v_ref, kv_ref, sems):
    width = k_ref.shape[1]
    copies = [
        pltpu.make_async_copy(src, kv_ref.at[:, pl.ds(i * width, width)], sems.at[i])
        for i, src in enumerate((k_ref, v_ref))
    ]
    for copy in copies:
        copy.start()
    for copy in copies:
        copy.wait()


def choose(place_ref, kv_ref, before_ref, *outs):
    for bit, out in zip((4, 2, 1), outs, strict=True):
        ahead = (place_ref[0] & bit) == 0

        @pl.when(ahead)
        def _():
            out[...] = kv_ref[...]

        @pl.when(jnp.logical_not(ahead))
        def _():
            out[...] = before_ref[...]


def finish(place_ref, own_ref, far_refs, last_refs, key_ref, value_ref):
    width = key_ref.shape[1]
    key_ref[...] = own_ref[:, :width]
    value_ref[...] = own_ref[:, width:]

    def add(refs):
        key_ref[...] += sum(r[:, :width].astype(F32) for r in refs)
        value_ref[...] += sum(r[:, width:].astype(F32) for r in refs)

    for bits, refs in far_refs:
        pl.when((place_ref[0] & bits) == 0)(functools.partial(add, refs))
    add(last_refs)


def document_starts(me_ref, seg_ref, start_ref, first_ref):
    lanes = seg_ref.shape[1]
    tok = start_ref.shape[1]
    base = pl.multiple_of(me_ref[0] * (tok // lanes), tok // lanes)
    row = jnp.concatenate([seg_ref[pl.ds(base + j, 1), :] for j in range(tok // lanes)], axis=1)
    grid = jnp.broadcast_to(row, (tok, tok))
    inside = jnp.sum((grid.T < grid).astype(jnp.int32), axis=0, keepdims=True)
    head = jnp.sum((seg_ref[...] < row[0, 0]).astype(jnp.int32)) - me_ref[0] * tok
    start_ref[...] = jnp.where(inside > 0, inside, head)
    first_ref[0] = head


def tile_views(ctx, place, bit):
    if bit == OWN:
        return 0
    back = ((place - (place ^ bit) + 2 * REACH - 1) & (REACH - 1)) + 1
    return -back * ctx.tok


class Sizes:
    def __init__(self, heads, tok, width):
        self.heads, self.tok, self.width = heads, tok, width
        self.rows = heads * tok
        self.scale = width**-0.5
        self.c = self.scale * math.log2(math.e)

    def lanes(self, h):
        return slice(h * self.tok, (h + 1) * self.tok)

    def cols(self, h):
        return slice(h * self.width, (h + 1) * self.width)


def stack_heads(z, src, dst):
    for h in range(z.heads):
        dst[z.lanes(h), :] = src[:, z.cols(h)]


def masked(z, s, start_ref, rel, own):
    rows = lax.broadcasted_iota(jnp.int32, (z.tok, z.tok), 0)
    ok = rows >= start_ref[0:1, :] - rel
    if own:
        ok = ok & (rows <= lax.broadcasted_iota(jnp.int32, (z.tok, z.tok), 1))
    return jnp.where(ok, s, NEG)


def backward_tile(z, tile, prob, qs, gs, delta, p_buf, d_buf, dq_acc):
    v = tile[:, z.width :]
    kt = tile[:, : z.width].T
    for h in range(z.heads):
        lanes = z.lanes(h)
        p = prob(h)
        dp = dot(v, gs[lanes, :], NT)
        d_buf[:, lanes] = (p * (dp - delta[0:1, lanes])).astype(BF)
        p_buf[:, lanes] = p.astype(BF)
    dv = dot(p_buf[...], gs[...])
    dk = dot(d_buf[...], qs[...]) * z.scale
    dq_acc[...] += dot(kt, d_buf[...])
    return dk, dv


def forward_kernel(z, order, fresh, early, *refs):
    refs = list(refs)
    place_ref, first_ref, pong, q_ref = refs[:4]
    g_ref = refs.pop(4) if early else None
    start_ref = refs[4]
    n = len(order)
    at = 5
    if not fresh:
        old_top, old_total, old_acc = refs[at : at + 3]
        at += 3
    kv_refs = refs[at : at + n]
    at += n
    if early:
        out_ref, top, delta, dq_acc = refs[at : at + 4]
        at += 4
        part_refs = refs[at : at + early]
        at += early
        total, acc, gs, d_buf = refs[at : at + 4]
        at += 4
    else:
        top, total, acc = refs[at : at + 3]
        at += 3
    qs, p_buf, tiles, s_buf = refs[at:]
    groups = z.tok // 8
    loop = n - 1 if fresh else n
    stack_heads(z, q_ref, qs)
    for i in range(n):
        tiles[i] = kv_refs[i][...]

    def scores(i, rel, own):
        k = tiles[i, :, : z.width]
        for h in range(z.heads):
            lanes = z.lanes(h)
            s = masked(z, dot(k, qs[lanes, :], NT) * z.c, start_ref, rel, own)
            s_buf[i, :, lanes] = s
            m = jnp.max(s.reshape(groups, 8, z.tok), axis=0)
            top[:, lanes] = m if own else jnp.maximum(top[:, lanes], m)

    def forward(i, own):
        vt = tiles[i, :, z.width :].T
        for h in range(z.heads):
            lanes = z.lanes(h)
            p = jnp.exp2(s_buf[i, :, lanes] - top[0:1, lanes])
            t = jnp.sum(p.reshape(groups, 8, z.tok), axis=0)
            p_buf[:, lanes] = p.astype(BF)
            total[:, lanes] = t if own else total[:, lanes] + t
        o = dot(vt, p_buf[...])
        acc[...] = o if own else acc[...] + o

    place = place_ref[0]
    rels = [tile_views(z, place, bit) for bit in order]

    def each_seen(visit):
        def step(i, carry):
            rel = rels[0]
            for j in range(1, loop):
                rel = jnp.where(i == j, rels[j], rel)

            @pl.when(rel + z.tok > first_ref[0])
            def _():
                visit(i, rel)

            return carry

        lax.fori_loop(0, loop, step, 0)

    if fresh:
        scores(n - 1, 0, True)
    else:
        top[...] = jnp.broadcast_to(old_top[0:1, :], top.shape)
    each_seen(lambda i, rel: scores(i, rel, False))
    top[0:1, :] = jnp.max(top[...], axis=0, keepdims=True)
    if fresh:
        forward(n - 1, True)
    else:
        alpha = jnp.exp2(old_top[0:1, :] - top[0:1, :])
        total[...] = old_total[...] * alpha
        acc[...] = old_acc[...] * alpha
    each_seen(lambda i, rel: forward(i, False))
    if not early:
        return

    for h in range(z.heads):
        lanes = z.lanes(h)
        sums = jnp.sum(total[:, lanes], axis=0, keepdims=True)
        o = (acc[:, lanes] * (1.0 / sums)).astype(BF).T
        out_ref[:, z.cols(h)] = o
        prod = g_ref[:, z.cols(h)].astype(F32) * o.astype(F32)
        delta[0:1, lanes] = jnp.sum(prod.T, axis=0, keepdims=True)
        top[0:1, lanes] = top[0:1, lanes] + jnp.log2(sums)

    dq_acc[...] = jnp.zeros_like(dq_acc)
    for part in part_refs:
        part[...] = jnp.zeros_like(part)

    @pl.when(pong[0] == 1)
    def _():
        stack_heads(z, g_ref, gs)
        for i in range(early):

            @pl.when(rels[i] + z.tok > first_ref[0])
            def _():
                def prob(h):
                    return jnp.exp2(s_buf[i, :, z.lanes(h)] - top[0:1, z.lanes(h)])

                dk, dv = backward_tile(z, kv_refs[i], prob, qs, gs, delta, p_buf, d_buf, dq_acc)
                part_refs[i][:, : z.width] = dk.astype(BF)
                part_refs[i][:, z.width :] = dv.astype(BF)


def backward_kernel(z, order, last, *refs):
    place_ref, first_ref, pong = refs[:3]
    q_ref, g_ref, start_ref, top, delta, dq_in = refs[3:9]
    n = len(order)
    kv_refs = refs[9 : 9 + n]
    out_ref = refs[9 + n]
    part_refs = refs[10 + n : 10 + 2 * n]
    qs, gs, p_buf, d_buf = refs[10 + 2 * n : 14 + 2 * n]
    dq_acc = refs[14 + 2 * n] if last else out_ref
    place = place_ref[0]

    @pl.when(pong[0] == 1)
    def _():
        stack_heads(z, q_ref, qs)
        stack_heads(z, g_ref, gs)
        dq_acc[...] = dq_in[...]
        for i, bit in enumerate(order):
            rel = tile_views(z, place, bit)
            seen = rel + z.tok > first_ref[0]

            @pl.when(seen)
            def _():
                def prob(h):
                    s = dot(kv_refs[i][:, : z.width], qs[z.lanes(h), :], NT) * z.c
                    s = masked(z, s, start_ref, rel, bit == OWN)
                    return jnp.exp2(s - top[0:1, z.lanes(h)])

                dk, dv = backward_tile(z, kv_refs[i], prob, qs, gs, delta, p_buf, d_buf, dq_acc)
                part_refs[i][:, : z.width] = dk.astype(part_refs[i].dtype)
                part_refs[i][:, z.width :] = dv.astype(part_refs[i].dtype)

            @pl.when(jnp.logical_not(seen))
            def _():
                part_refs[i][...] = jnp.zeros_like(part_refs[i])

        if last:
            for h in range(z.heads):
                out_ref[:, z.cols(h)] = (dq_acc[:, z.lanes(h)] * z.scale).astype(BF).T

    @pl.when(pong[0] != 1)
    def _():
        out_ref[...] = jnp.zeros_like(out_ref)
        for part in part_refs:
            part[...] = jnp.zeros_like(part)


def cost(z, tiles, products):
    pairs = z.rows * tiles * z.tok
    return pl.CostEstimate(
        flops=2 * products * pairs * z.width, bytes_accessed=6 << 20, transcendentals=pairs
    )


def run_forward(z, scalars, queries, out_grad, start, state, tiles, order, early):
    n = len(order)
    shape = jax.ShapeDtypeStruct
    stats, wide = shape((8, z.rows), F32), shape((z.width, z.rows), F32)
    scratch = [
        pltpu.VMEM((z.rows, z.width), BF),
        pltpu.VMEM((z.tok, z.rows), BF),
        pltpu.VMEM((n, z.tok, 2 * z.width), BF),
        pltpu.VMEM((n, z.tok, z.rows), F32),
    ]
    if early:
        outs = [shape(queries.shape, BF), stats, stats, wide] + [shape((z.tok, 2 * z.width), BF)] * early
        scratch = [
            pltpu.VMEM((8, z.rows), F32),
            pltpu.VMEM((z.width, z.rows), F32),
            pltpu.VMEM((z.rows, z.width), BF),
            pltpu.VMEM((z.tok, z.rows), BF),
        ] + scratch
    else:
        outs = [stats, stats, wide]
    args = [queries, out_grad, start] if early else [queries, start]
    args += list(state) + list(tiles)
    return pl.pallas_call(
        functools.partial(forward_kernel, z, order, not state, early),
        out_shape=outs,
        in_specs=[SMEM] * 3 + [VMEM] * len(args),
        out_specs=[VMEM] * len(outs),
        scratch_shapes=scratch,
        compiler_params=room(24 if early else 16),
        cost_estimate=cost(z, n, 4),
    )(*scalars, *args)


def run_backward(z, scalars, queries, out_grad, start, state, tiles, order, last):
    n = len(order)
    shape = jax.ShapeDtypeStruct
    dq = shape(queries.shape, BF) if last else shape((z.width, z.rows), F32)
    parts = [shape((z.tok, 2 * z.width), F32 if bit == OWN else BF) for bit in order]
    return pl.pallas_call(
        functools.partial(backward_kernel, z, order, last),
        out_shape=[dq] + parts,
        in_specs=[SMEM] * 3 + [VMEM] * (6 + n),
        out_specs=[VMEM] * (1 + n),
        scratch_shapes=[
            pltpu.VMEM((z.rows, z.width), BF),
            pltpu.VMEM((z.rows, z.width), BF),
            pltpu.VMEM((z.tok, z.rows), BF),
            pltpu.VMEM((z.tok, z.rows), BF),
        ]
        + ([pltpu.VMEM((z.width, z.rows), F32)] if last else []),
        compiler_params=room(10),
        cost_estimate=cost(z, n, 10),
    )(*scalars, queries, out_grad, start, *state, *tiles)


def on_device(queries, key_vectors, value_vectors, out_grad, segments, phase_label):
    tok, width = key_vectors.shape
    z = Sizes(queries.shape[1] // width, tok, width)
    devices = lax.axis_size(AXES)
    me = lax.axis_index(AXES).astype(jnp.int32)
    place = me & (REACH - 1)
    shape = jax.ShapeDtypeStruct
    block = shape((tok, 2 * width), BF)

    def swap(x, bit):
        return lax.ppermute(x, AXES, [(i, i ^ bit) for i in range(devices)])

    def shift(x, by):
        pairs = [(i, i + by) for i in range(devices) if 0 <= i + by < devices]
        return lax.ppermute(x, AXES, pairs)

    def give_back(x, bit):
        pairs = [(i, i ^ bit if i & bit else (i ^ bit) - REACH) for i in range(devices)]
        return lax.ppermute(x, AXES, [(i, j) for i, j in pairs if j >= 0])

    kv = pl.pallas_call(
        pack_pair,
        out_shape=block,
        in_specs=[pl.BlockSpec(memory_space=pltpu.HBM)] * 2,
        out_specs=VMEM,
        scratch_shapes=[pltpu.SemaphoreType.DMA((2,))],
        compiler_params=room(4),
    )(key_vectors, value_vectors)
    before = shift(kv, REACH)
    start, first = pl.pallas_call(
        document_starts,
        out_shape=[shape((1, tok), jnp.int32), shape((1,), jnp.int32)],
        in_specs=[SMEM, VMEM],
        out_specs=[VMEM, SMEM],
        compiler_params=room(4),
    )(me[None], segments.reshape(-1, 128))
    before, start, first = lax.optimization_barrier((before, start, first))
    ahead = pl.pallas_call(
        choose, out_shape=[block] * 3, in_specs=[SMEM] + [VMEM] * 2, out_specs=[VMEM] * 3, compiler_params=room(4)
    )(place[None], kv, before)
    slot = {0: before, 4: swap(ahead[0], 4), 2: swap(ahead[1], 2)}
    slot[1] = swap(ahead[2], 1)
    scalars = (place[None], first, phase_label)
    slot[OWN] = kv

    def more(state, near):
        return run_forward(z, scalars, queries, None, start, state, [slot[b] for b in near], near, 0)

    slot[4], *state = lax.optimization_barrier((slot[4], *more((), NEAR[0])))
    slot[5] = swap(slot[4], 1)
    slot[6] = swap(slot[4], 2)
    slot[3] = swap(slot[2], 1)
    slot[7] = swap(slot[5], 2)
    state = more(state, NEAR[1])
    order = (5, 7, 3, 6)
    attn_out, top, delta, dq, *parts = run_forward(
        z, scalars, queries, out_grad, start, state, [slot[b] for b in order], order, 3
    )
    part = dict(zip(order[:3], parts, strict=True))
    got = {b: swap(part[b ^ 1], 1) for b in (2, 6, 4)}
    some = (4, 6, 2)
    dq, *parts = run_backward(
        z, scalars, queries, out_grad, start, (top, delta, dq), [slot[b] for b in some], some, False
    )
    part.update(zip(some, parts, strict=True))

    def pair(bit):
        return (part[bit].astype(F32) + got[bit].astype(F32)).astype(BF)

    came = {4: swap(pair(4), 4), 6: swap(pair(6), 6)}
    dq, near_pair = lax.optimization_barrier((dq, pair(2)))
    came[2] = swap(near_pair, 2)
    rest = (1, 0, OWN)
    grad_query, *parts = run_backward(
        z, scalars, queries, out_grad, start, (top, delta, dq), [slot[b] for b in rest], rest, True
    )
    part.update(zip(rest, parts, strict=True))
    others = part[0].astype(F32)
    for bits in ((4, 6), (2,)):
        total = sum(came[b].astype(F32) for b in bits)
        others = others + jnp.where((place & bits[0]) == 0, 0.0, total)
    last = [give_back(part[1], 1), shift(others.astype(BF), -REACH)]
    grad_key, grad_value = pl.pallas_call(
        lambda place_ref, own, c4, c6, c2, l1, l0, *outs: finish(
            place_ref, own, ((4, (c4, c6)), (2, (c2,))), (l1, l0), *outs
        ),
        out_shape=[shape((tok, width), F32)] * 2,
        in_specs=[SMEM] + [VMEM] * 6,
        out_specs=[VMEM] * 2,
        compiler_params=room(4),
    )(place[None], part[OWN], came[4], came[6], came[2], *last)
    return (attn_out, grad_query, grad_key, grad_value)


def solution(mesh):
    rows = P(AXES, None)
    return jax.shard_map(
        on_device,
        mesh=mesh,
        in_specs=(rows, rows, rows, rows, P(), P(AXES)),
        out_specs=(rows, rows, rows, rows),
        check_vma=False,
    )
```
